256 devices in a mesh: head: 16 (over y_hi, z), blk: 16 (over x, y_lo, core).
Axes of the slice: x: 4, y: 4 (y_hi: 2, y_lo: 2; y = y_hi * 2 + y_lo), z: 8, core: 2. Of those that a mesh axis runs over, the one named last changes fastest.
Arguments:
- hidden: bfloat16 [12288, 3072], P(('blk', 'head')), may hold values from -6 to 6
- cotangent: bfloat16 [12288, 3072], P(('blk', 'head')), may hold values from -6 to 6
- step_index: int32 [1], replicated, may hold values from 0 to 31
- mod_table: float32 [32, 3, 3072], replicated, may hold values from -3 to 3
- w_qkv: bfloat16 [3072, 16, 384], P(None, 'head'), may hold values from -0.109375 to 0.109375
- qk_gains: float32 [2, 128], replicated, may hold values from 0.6 to 2.4
- w_out: bfloat16 [16, 128, 3072], P('head'), may hold values from -0.125 to 0.125
- tile_pairs: int32 [16, 3], replicated, may hold values from -1 to 15, as said below
- tile_owner: int32 [16], replicated, may hold values from 0 to 15, each once
Outputs:
- result: bfloat16 [12288, 3072], P(('blk', 'head'))
- grad_hidden: bfloat16 [12288, 3072], P(('blk', 'head'))
The draws below stay inside these ranges and needn't reach their ends.
Inputs may be any that keep to these rules, and one draw needn't show every extreme that they name: `tile_pairs`: row t lists first t itself, then none, one or both of (t - 1) mod 16 and (t + 1) mod 16, each at most once; unused slots hold -1 and come last.
All inputs are finite; a program needn't handle non-finite values.
Results may differ from the reference program's by a relative error of at most 0.024.
Values may be sent and summed in bfloat16 or wider, within the bound.
A program may use at most 128 MiB of HBM per device.

```python
import math
import jax
import jax.numpy as jnp
from jax import lax

D = 3072
HEADS = 16
HD = 128
TILE = 768
NB = 3
STEPS = 32
TILES_BLK = 1
TILES = 16
TOKENS = 12288
HEADS_DEV = 1
N_BLK = 16


def draw_qk_gains(key, part):
    return jnp.exp(jax.random.uniform(key, (2, HD), jnp.float32, math.log(0.6), math.log(1.6)))


def draw_tile_pairs(key, part):
    first_key, second_key = jax.random.split(jax.random.fold_in(key, 17))
    places = jnp.arange(TILES, dtype=jnp.int32)
    counts = jax.random.randint(first_key, (TILES,), 1, NB + 1)
    counts = counts.at[0].set(NB)
    counts = counts.at[1].set(1)
    flips = jax.random.randint(second_key, (TILES,), 0, 2)
    upper = (places + 1) % TILES
    lower = (places + TILES - 1) % TILES
    second = jnp.where(flips == 1, upper, lower)
    third = jnp.where(flips == 1, lower, upper)
    table = jnp.stack([places, second, third], axis=1)
    slots = jnp.arange(NB, dtype=jnp.int32)[None, :]
    return jnp.where(slots < counts[:, None], table, -1).astype(jnp.int32)


def shard_levels(rng, extent, shards, low, high):
    factor_of, own = 1.0, jax.random.fold_in(rng, 6)
    for dim, shards_of in shards:
        steps = jnp.exp(jax.random.uniform(jax.random.fold_in(own, dim), (shards_of,), jnp.float32, low / len(shards), high / len(shards)))
        factor_of = factor_of * jnp.repeat(steps, extent[dim] // shards_of).reshape([-1 if axis == dim else 1 for axis in range(len(extent))])
    return factor_of


def noise(rng, extent, scale, limit, cuts=(), held_as=jnp.bfloat16):
    values = scale * jax.random.normal(rng, extent, jnp.float32)
    if cuts:
        values = values * shard_levels(rng, extent, cuts, -0.22, 0.18)
    return jnp.clip(values, -limit, limit).astype(held_as)


def setup_inputs(seed: int = 0) -> dict:
    key_of = jax.random.split(jax.random.key(seed), 10)
    return {
        "hidden": noise(key_of[0], (TOKENS, D), 1.0, 6.0, ((0, 256),)),
        "cotangent": noise(key_of[1], (TOKENS, D), 1.0, 6.0, ((0, 256),)),
        "step_index": jax.random.randint(key_of[2], (1,), 0, STEPS).astype(jnp.int32),
        "mod_table": noise(key_of[3], (STEPS, 3, D), 0.5, 3.0, (), jnp.float32),
        "w_qkv": noise(key_of[4], (D, HEADS, 3 * HD), D ** -0.5, 0.109375, ((1, 16),)),
        "qk_gains": draw_qk_gains(jax.random.fold_in(key_of[9], 71), 0),
        "w_out": noise(key_of[6], (HEADS, HD, D), (HEADS * HD) ** -0.5, 0.125, ((0, 16),)),
        "tile_pairs": draw_tile_pairs(jax.random.fold_in(key_of[9], 71), 0),
        "tile_owner": jax.random.permutation(key_of[8], TILES).astype(jnp.int32),
    }


EPS = 1e-06
NEG = -1e+30

def rounded(values):
    return lax.optimization_barrier(values.astype(jnp.bfloat16)).astype(jnp.float32)

def layer_norm(rows):
    rows = rows.astype(jnp.float32)
    center = rows - lax.optimization_barrier(jnp.mean(rows, axis=-1, keepdims=True))
    spread = lax.optimization_barrier(jnp.mean(center * center, axis=-1, keepdims=True))
    return center * lax.rsqrt(spread + EPS)

def modulate(rows, shift, scale):
    return layer_norm(rows) * (1.0 + scale) + shift

def rms_gain(source, gain):
    return source * lax.rsqrt(lax.optimization_barrier(jnp.mean(source * source, axis=-1, keepdims=True)) + EPS) * gain

def inverse_positions(tile_owner):
    count = tile_owner.shape[0]
    places = jnp.arange(count, dtype=jnp.int32)
    match = tile_owner[None, :] == places[:, None]
    return lax.optimization_barrier(jnp.sum(jnp.where(match, places[None, :], 0), axis=1)).astype(jnp.int32)

def listed_keys(keys, values, listed, inverse, tile_rows):
    key_parts, value_parts, flags = ([], [], [])
    for number in range(listed.shape[0]):
        entry = listed[number]
        begin = (inverse[jnp.maximum(entry, 0)] * tile_rows).astype(jnp.int32)
        key_parts.append(lax.dynamic_slice_in_dim(keys, begin, tile_rows, 0))
        value_parts.append(lax.dynamic_slice_in_dim(values, begin, tile_rows, 0))
        flags.append(jnp.broadcast_to(entry >= 0, (tile_rows,)))
    return (jnp.concatenate(key_parts, 0), jnp.concatenate(value_parts, 0), jnp.concatenate(flags, 0))

def tile_attention(query, keys, values, valid, factor):
    scores = jnp.einsum('qhd,khd->hqk', query.astype(jnp.float32), keys.astype(jnp.float32)) * factor
    scores = jnp.where(valid[None, None, :], scores, NEG)
    expos = jnp.exp(scores)
    total = lax.optimization_barrier(jnp.sum(expos, axis=-1))
    prob_low = (expos / total[..., None]).astype(jnp.bfloat16)
    attended = jnp.einsum('hqk,khd->qhd', prob_low.astype(jnp.float32), values.astype(jnp.float32))
    return (attended.astype(jnp.bfloat16), total)

def tile_backward(query, keys, values, valid, d_out, total, delta, factor):
    scores = jnp.einsum('qhd,khd->hqk', query.astype(jnp.float32), keys.astype(jnp.float32)) * factor
    scores = jnp.where(valid[None, None, :], scores, NEG)
    prob = jnp.exp(scores) / total[..., None]
    d_prob = jnp.einsum('qhd,khd->hqk', d_out.astype(jnp.float32), values.astype(jnp.float32))
    d_score = (prob * (d_prob - delta[..., None])).astype(jnp.bfloat16).astype(jnp.float32)
    prob_low = prob.astype(jnp.bfloat16).astype(jnp.float32)
    d_query = jnp.einsum('hqk,khd->qhd', d_score, keys.astype(jnp.float32)) * factor
    d_keys = jnp.einsum('hqk,qhd->khd', d_score, query.astype(jnp.float32)) * factor
    d_values = jnp.einsum('hqk,qhd->khd', prob_low, d_out.astype(jnp.float32))
    return (d_query, jnp.concatenate([d_keys, d_values], -1))

def reference(hidden, cotangent, step_index, mod_table, w_qkv, qk_gains, w_out, tile_pairs, tile_owner):
    factor = HD ** (-0.5)
    mods = lax.dynamic_index_in_dim(mod_table, step_index[0], 0, keepdims=False)
    shift, scale, gate = (mods[0], mods[1], mods[2])

    def modulate_rows(rows):
        return modulate(rows, shift, scale)

    def query_norm(source):
        return rms_gain(source, qk_gains[0])

    def keys_norm(source):
        return rms_gain(source, qk_gains[1])
    hidden_wide = hidden.astype(jnp.float32)
    modulated = modulate_rows(hidden_wide).astype(jnp.bfloat16)
    w_flat = w_qkv.reshape(D, HEADS * 3 * HD)
    projected = jnp.dot(modulated, w_flat, preferred_element_type=jnp.float32).reshape(TOKENS, HEADS, 3 * HD)
    raw_query = projected[..., :HD]
    raw_keys = projected[..., HD:2 * HD]
    query = query_norm(raw_query).astype(jnp.bfloat16)
    keys = keys_norm(raw_keys).astype(jnp.bfloat16)
    values = projected[..., 2 * HD:].astype(jnp.bfloat16)
    inverse = inverse_positions(tile_owner)

    def forward_tile(position):
        tile = tile_owner[position]
        chosen_keys, chosen_values, valid = listed_keys(keys, values, tile_pairs[tile], inverse, TILE)
        rows_query = lax.dynamic_slice_in_dim(query, (position * TILE).astype(jnp.int32), TILE, 0)
        return tile_attention(rows_query, chosen_keys, chosen_values, valid, factor)
    outs, totals = lax.map(forward_tile, jnp.arange(TILES, dtype=jnp.int32))
    attended = outs.reshape(TOKENS, HEADS, HD)
    groups = HEADS // HEADS_DEV
    attended_groups = attended.reshape(TOKENS, groups, HEADS_DEV * HD)
    w_out_groups = w_out.reshape(groups, HEADS_DEV * HD, D)

    def add_group(index, summed):
        part = jnp.dot(lax.dynamic_index_in_dim(attended_groups, index, 1, keepdims=False), lax.dynamic_index_in_dim(w_out_groups, index, 0, keepdims=False), preferred_element_type=jnp.float32)
        return summed + rounded(part)
    proj = lax.fori_loop(0, groups, add_group, jnp.zeros((TOKENS, D), jnp.float32))
    result = (hidden_wide + gate * proj).astype(jnp.bfloat16)
    d_proj = (cotangent.astype(jnp.float32) * gate).astype(jnp.bfloat16)
    d_attended = lax.dot_general(d_proj, w_out.reshape(HEADS * HD, D), (((1,), (1,)), ((), ())), preferred_element_type=jnp.float32)
    d_attended = d_attended.astype(jnp.bfloat16).reshape(TOKENS, HEADS, HD)

    def slab_step(slab, carry):
        grads, d_query_all = carry
        term = jnp.zeros((TOKENS, HEADS, 2 * HD), jnp.float32)
        for local in range(TILES_BLK):
            position = (slab * TILES_BLK + local).astype(jnp.int32)
            tile = tile_owner[position]
            listed = tile_pairs[tile]
            chosen_keys, chosen_values, valid = listed_keys(keys, values, listed, inverse, TILE)
            begin = (position * TILE).astype(jnp.int32)
            rows_query = lax.dynamic_slice_in_dim(query, begin, TILE, 0)
            rows_out = lax.dynamic_slice_in_dim(attended, begin, TILE, 0)
            rows_grad = lax.dynamic_slice_in_dim(d_attended, begin, TILE, 0)
            total = lax.dynamic_index_in_dim(totals, position, 0, keepdims=False)
            delta = lax.optimization_barrier(jnp.sum(rows_grad.astype(jnp.float32) * rows_out.astype(jnp.float32), axis=-1)).T
            d_query, pieces = tile_backward(rows_query, chosen_keys, chosen_values, valid, rows_grad, total, delta, factor)
            d_query_all = lax.dynamic_update_slice_in_dim(d_query_all, d_query, begin, 0)
            for number in range(NB):
                entry = listed[number]
                place = (inverse[jnp.maximum(entry, 0)] * TILE).astype(jnp.int32)
                before = lax.dynamic_slice_in_dim(term, place, TILE, 0)
                term = lax.dynamic_update_slice_in_dim(term, before + pieces[number * TILE:(number + 1) * TILE], place, 0)
        return (grads + rounded(term), d_query_all)
    start_grads = jnp.zeros((TOKENS, HEADS, 2 * HD), jnp.float32)
    start_query = jnp.zeros((TOKENS, HEADS, HD), jnp.float32)
    grads, d_query_all = lax.fori_loop(0, N_BLK, slab_step, (start_grads, start_query))
    _, pull_query = jax.vjp(query_norm, raw_query)
    d_raw_query, = pull_query(d_query_all)
    _, pull_keys = jax.vjp(keys_norm, raw_keys)
    d_raw_keys, = pull_keys(grads[..., :HD])
    d_projected = jnp.concatenate([d_raw_query, d_raw_keys, grads[..., HD:]], -1).astype(jnp.bfloat16)
    d_projected = d_projected.reshape(TOKENS, groups, HEADS_DEV * 3 * HD)
    w_groups = w_qkv.reshape(D, groups, HEADS_DEV * 3 * HD)

    def add_back(index, summed):
        part = lax.dot_general(lax.dynamic_index_in_dim(d_projected, index, 1, keepdims=False), lax.dynamic_index_in_dim(w_groups, index, 1, keepdims=False), (((1,), (1,)), ((), ())), preferred_element_type=jnp.float32)
        return summed + rounded(part)
    d_modulated = lax.fori_loop(0, groups, add_back, jnp.zeros((TOKENS, D), jnp.float32))
    _, pull_rows = jax.vjp(modulate_rows, hidden_wide)
    d_input, = pull_rows(d_modulated)
    grad_hidden = (cotangent.astype(jnp.float32) + d_input).astype(jnp.bfloat16)
    return (result, grad_hidden)
```

```python
import functools

import jax
import jax.numpy as jnp
from jax import lax
from jax.experimental import pallas as pl
from jax.experimental.pallas import tpu as pltpu
from jax.sharding import PartitionSpec as P

EPS = 1e-6
TILE = 768
HD = 128
D = 3072
HALF = D // 2
SUB = 48
CH = 96
NZ = 8
F32 = jnp.float32
BF16 = jnp.bfloat16
FACTOR = HD ** -0.5
LOG2E = 1.4426950408889634
MESH = pl.DeviceIdType.MESH
NT = (((1,), (1,)), ((), ()))
TN = (((0,), (0,)), ((), ()))


def dot(a, b, dims=(((1,), (0,)), ((), ()))):
    return lax.dot_general(a, b, dims, preferred_element_type=F32)


def kernel(
    hid, cot, mods, wqkv, gains, wout, pairs, owner,
    res_out, gh_out,
    xs, cs, xg, cg, wq, wo, raw, psend, precv, dsend, drecv,
    qa, ka, va, doa, sta, attb, dqb, ot, dqt, dk, dv,
    rsnd, rrcv, rfin, ret,
    s_cross, r_cross, s_w, r_w, l_w, s_z, r_z, s_core, r_core,
    s_pl, r_pl, s_rs, r_rs, s_ret, r_ret,
):
    head, blk = lax.axis_index("head"), lax.axis_index("blk")
    yh, z = head // 8, lax.rem(head, 8)
    x, yl, c = blk // 4, lax.rem(blk // 2, 2), lax.rem(blk, 2)
    y = yh * 2 + yl

    def dev(yh=yh, z=z, x=x, yl=yl, c=c):
        return (yh * 8 + z, (x * 2 + yl) * 2 + c)

    def at_y(yy):
        yy = lax.rem(yy + 4, 4)
        return dev(yh=yy // 2, yl=lax.rem(yy, 2))

    def at_x(xx):
        return dev(x=lax.rem(xx + 4, 4))

    def at_z(zz):
        return dev(z=lax.rem(zz + 8, 8))

    sibling = dev(c=1 - c)
    wpartner = dev(yh=1 - yh, yl=1 - yl)
    own = c == yh

    barrier = pltpu.get_barrier_semaphore()
    partners = [
        at_x(x + 1), at_x(x - 1), at_y(y + 1), at_y(y - 1), at_z(z + 1), at_z(z - 1),
        sibling, dev(yh=1 - yh), dev(yh=1 - yh, c=1 - c),
    ]
    for p in partners:
        pl.semaphore_signal(barrier, inc=1, device_id=p, device_id_type=MESH)

    shift = mods[0:1, :]
    scale = mods[1:2, :]
    gate = mods[2:3, :]

    def normed():
        rows = hid[...].astype(F32)
        center = rows - jnp.mean(rows, axis=-1, keepdims=True)
        spread = jnp.mean(center * center, axis=-1, keepdims=True)
        r = lax.rsqrt(spread + EPS)
        return center * r, r

    hat, _ = normed()
    xs[...] = (hat * (1.0 + scale) + shift).astype(BF16)
    cs[...] = (cot[...].astype(F32) * gate).astype(BF16)

    pl.semaphore_wait(barrier, len(partners))

    def remote(src, dst, ss, rs, target):
        return pltpu.make_async_remote_copy(
            src_ref=src, dst_ref=dst, send_sem=ss, recv_sem=rs,
            device_id=target, device_id_type=MESH,
        )

    pending = []

    def send(src, dst, ss, rs, target):
        copy = remote(src, dst, ss, rs, target)
        copy.start()
        pending.append(copy.wait_send)

    def arrived(dst, rs):
        remote(dst, dst, rs, rs, sibling).wait_recv()

    def rows_of(zz, sub, count=SUB):
        return pl.ds(pl.multiple_of(zz * CH + sub * SUB, 16), count)

    def cross_send(n, stage, grid):
        for h in range(2):
            src = stage.at[:, h * HALF:(h + 1) * HALF]
            dst = grid.at[rows_of(z, yh)]
            here = jnp.logical_and(own, c == h)

            @pl.when(here)
            def _():
                pltpu.make_async_copy(src, dst, r_cross.at[n, yh]).start()

            copy = remote(src, dst, s_cross.at[n, h], r_cross.at[n, yh], dev(yh=c, c=h))

            @pl.when(jnp.logical_not(here))
            def _():
                copy.start()

            def done(here=here, copy=copy):
                @pl.when(jnp.logical_not(here))
                def _():
                    copy.wait_send()
            pending.append(done)

    def cross_wait(n, grid):
        for sub in range(2):
            dst = grid.at[rows_of(z, sub)]
            pltpu.make_async_copy(dst, dst, r_cross.at[n, sub]).wait()

    cross_send(0, xs, xg)
    wq_src = wqkv.at[pl.ds(pl.multiple_of(c * HALF, 16), HALF)]
    wq_dst = wq.at[:, pl.ds(pl.multiple_of(yh * 384, 128), 384)]
    wo_src = wout.at[:, pl.ds(pl.multiple_of(c * HALF, 128), HALF)]
    wo_dst = wo.at[pl.ds(pl.multiple_of(yh * HD, 16), HD)]
    send(wq_src, wq_dst, s_w.at[0], r_w.at[0], wpartner)
    wq_local = pltpu.make_async_copy(wq_src, wq_dst, l_w.at[0])
    wq_local.start()
    wo_local = pltpu.make_async_copy(wo_src, wo_dst, l_w.at[1])
    wo_local.start()
    cross_send(1, cs, cg)
    send(wo_src, wo_dst, s_w.at[1], r_w.at[1], wpartner)

    def z_piece(j, sign, off):
        chunk = lax.rem(z + off + 16, 8)
        if j < 4:
            return rows_of(chunk, 0, CH)
        return rows_of(chunk, 0 if sign > 0 else 1)

    def z_start(n, grid, j):
        for i, sign in enumerate((1, -1)):
            ref = grid.at[z_piece(j, sign, -sign * (j - 1))]
            k = (j - 1) * 2 + i
            send(ref, ref, s_z.at[n, k], r_z.at[n, k], at_z(z + sign))

    def z_wait(n, grid, j):
        for i, sign in enumerate((1, -1)):
            arrived(grid.at[z_piece(j, sign, -sign * j)], r_z.at[n, (j - 1) * 2 + i])

    cross_wait(0, xg)
    z_start(0, xg, 1)
    z_wait(0, xg, 1)
    z_start(0, xg, 2)
    z_wait(0, xg, 2)
    z_start(0, xg, 3)
    z_wait(0, xg, 3)
    z_start(0, xg, 4)
    cross_wait(1, cg)
    z_start(1, cg, 1)
    z_wait(0, xg, 4)
    wq_local.wait()
    arrived(wq.at[:, pl.ds(pl.multiple_of((1 - yh) * 384, 128), 384)], r_w.at[0])

    def pick(first, second):
        return jnp.where(c == 0, first, second), jnp.where(c == 0, second, first)

    def qkv_rows(t, carry):
        r = pl.ds(pl.multiple_of(t * 256, 256), 256)
        part = dot(xg[r, :], wq[...])
        mine, other = pick(part[:, :384], part[:, 384:])
        raw[r, :] = mine
        psend[r, :] = other
        remote(psend.at[r], precv.at[r], s_core.at[t], r_core.at[t], sibling).start()
        return carry

    lax.fori_loop(0, 3, qkv_rows, 0)

    slot = x * 4 + y

    def rms(source, row):
        return lax.rsqrt(jnp.mean(source * source, axis=-1, keepdims=True) + EPS) * gains[row:row + 1, :]

    def norm_rows(t, carry):
        r = pl.ds(pl.multiple_of(t * 256, 256), 256)
        arrived(precv.at[r], r_core.at[t])
        total = raw[r, :] + precv[r, :]
        raw[r, :] = total
        query, key = total[:, :HD], total[:, HD:2 * HD]
        qa[slot, r, :] = (query * rms(query, 0)).astype(BF16)
        ka[slot, r, :] = (key * rms(key, 1)).astype(BF16)
        va[slot, r, :] = total[:, 2 * HD:].astype(BF16)
        return carry

    lax.fori_loop(0, 3, norm_rows, 0)

    def plane(n, ref, rows, swap):
        half = rows // 2

        def place(oa, ob):
            ox, oy = (ob, oa) if swap else (oa, ob)
            return lax.rem(x + ox + 4, 4) * 4 + lax.rem(y + oy + 4, 4)

        def target(axis, sign):
            on_x = (axis == 0) != swap
            return at_x(x + sign) if on_x else at_y(y + sign)

        moves = [(0, 1, 0, 0, None), (0, -1, 0, 0, None), (0, 1, -1, 0, 0), (0, -1, 1, 0, 1)]
        for oa in (0, -1, 1, -2):
            moves += [(1, 1, oa, 0, None), (1, -1, oa, 0, None), (1, 1, oa, -1, 0), (1, -1, oa, 1, 1)]

        def view(oa, ob, part):
            s = place(oa, ob)
            if part is None:
                return ref.at[s]
            return ref.at[s, pl.ds(part * half, half)]

        def start(*ids):
            for i in ids:
                axis, sign, oa, ob, part = moves[i]
                src = view(oa, ob, part)
                send(src, src, s_pl.at[n, i], r_pl.at[n, i], target(axis, sign))

        def wait(*ids):
            for i in ids:
                axis, sign, oa, ob, part = moves[i]
                if axis == 0:
                    oa = oa - sign
                else:
                    ob = ob - sign
                arrived(view(oa, ob, part), r_pl.at[n, i])

        def round_(k):
            if k == 1:
                start(0, 1, 4, 5)
            elif k == 2:
                wait(0, 1)
                start(2, 3, 8, 9, 12, 13)
                wait(4, 5)
                start(6, 7)
            elif k == 3:
                wait(2, 3)
                start(16, 17)
                wait(8, 9, 12, 13)
                start(10, 11, 14, 15)
            elif k == 4:
                wait(16, 17)
                start(18, 19)
            else:
                wait(6, 7, 10, 11, 14, 15, 18, 19)
        return round_

    k_round = plane(0, ka, TILE, False)
    v_round = plane(1, va, TILE, True)
    q_round = plane(2, qa, TILE, False)
    o_round = plane(3, doa, TILE, True)
    s_round = plane(4, sta, 16, False)

    k_round(1)
    v_round(1)
    z_wait(1, cg, 1)
    z_start(1, cg, 2)
    k_round(2)
    v_round(2)
    z_wait(1, cg, 2)
    z_start(1, cg, 3)
    k_round(3)
    v_round(3)
    z_wait(1, cg, 3)
    z_start(1, cg, 4)
    k_round(4)
    v_round(4)
    q_round(1)
    z_wait(1, cg, 4)
    wo_local.wait()
    arrived(wo.at[pl.ds(pl.multiple_of((1 - yh) * HD, 16), HD)], r_w.at[1])

    def grad_rows(t, carry):
        r = pl.ds(pl.multiple_of(t * 256, 256), 256)
        part = dot(cg[r, :], wo[...], NT)
        mine, other = pick(part[:, :HD], part[:, HD:])
        drecv[0, r, :] = mine
        dsend[r, :] = other
        return carry

    lax.fori_loop(0, 3, grad_rows, 0)
    send(dsend, drecv.at[1], s_core.at[3], r_core.at[3], sibling)
    k_round(5)
    v_round(5)
    arrived(drecv.at[1], r_core.at[3])
    doa[slot] = (drecv[0] + drecv[1]).astype(BF16)
    o_round(1)

    def position(s):
        return (s // 4 * 2 + s % 2) * 2 + (s % 4) // 2

    tile = owner[(x * 2 + yl) * 2 + yh]
    before = lax.rem(tile + 15, 16)
    after = lax.rem(tile + 1, 16)
    slot_b = jnp.int32(0)
    slot_a = jnp.int32(0)
    for s in range(16):
        o = owner[position(s)]
        slot_b = jnp.where(o == before, s, slot_b)
        slot_a = jnp.where(o == after, s, slot_a)

    def lists(a, b):
        hit = jnp.float32(0.0)
        for n in range(3):
            hit = jnp.where(pairs[a, n] == b, 1.0, hit)
        return hit

    one = jnp.float32(1.0)
    key_tiles = [(slot, one), (slot_b, lists(tile, before)), (slot_a, lists(tile, after))]
    query_tiles = [(slot_b, lists(before, tile)), (slot_a, lists(after, tile))]
    EXPC = FACTOR * LOG2E

    def scores(keys_, query_):
        return dot(keys_, query_, NT) * EXPC

    ot[...] = jnp.zeros_like(ot)
    total = jnp.zeros((1, TILE), F32)

    def attend(total, entry):
        s, valid = entry

        def block(t, total):
            r = pl.ds(pl.multiple_of(t * 256, 256), 256)
            e = jnp.exp2(scores(ka[s, r, :], qa[slot])) * valid
            ot[...] += dot(va[s, r, :], e.astype(BF16), TN)
            return total + jnp.sum(e, axis=0, keepdims=True)
        return lax.fori_loop(0, 3, block, total)

    total = attend(total, key_tiles[0])
    q_round(2)
    o_round(2)
    total = attend(total, key_tiles[1])
    q_round(3)
    o_round(3)
    total = attend(total, key_tiles[2])
    q_round(4)
    o_round(4)
    out_t = (ot[...] / total).astype(BF16).astype(F32)
    attb[c] = out_t.T.astype(BF16)
    send(attb.at[c], attb.at[c], s_core.at[4], r_core.at[4], sibling)
    lse = jnp.log2(total)
    delta = jnp.sum(out_t * doa[slot].astype(F32).T, axis=0, keepdims=True)
    for i in range(6):
        sta[slot, i:i + 1, :] = lse[:, i * HD:(i + 1) * HD]
        sta[slot, 8 + i:9 + i, :] = delta[:, i * HD:(i + 1) * HD]
    s_round(1)

    base = {4: 0, 3: SUB, 2: SUB + CH, 1: SUB + 2 * CH}

    def rs_step(n, partial, j):
        for i, sign in enumerate((1, -1)):
            dest = lax.rem(z + sign * j + 8, 8)
            k = (j - 1) * 2 + i
            if j == 4:
                value = partial(rows_of(dest, i))
                r = pl.ds(0, SUB)
            else:
                value = partial(rows_of(dest, 0, CH))
                r = pl.ds(base[j], CH)
                prev = pl.ds(base[j + 1], SUB if j == 3 else CH)
                arrived(rrcv.at[n, i, prev], r_rs.at[n, k + 2])
                got = rrcv[n, i, prev, :].astype(F32)
                if j == 3:
                    zero = jnp.zeros_like(got)
                    got = jnp.concatenate([got, zero] if i == 0 else [zero, got], axis=0)
                value = value + got
            rsnd[n, i, r, :] = value.astype(BF16)
            send(rsnd.at[n, i, r], rrcv.at[n, i, r], s_rs.at[n, k], r_rs.at[n, k], at_z(z + sign))

    def rs_finish(n, partial):
        value = partial(rows_of(z, 0, CH))
        r = pl.ds(base[1], CH)
        for i in range(2):
            arrived(rrcv.at[n, i, r], r_rs.at[n, i])
            value = value + rrcv[n, i, r, :].astype(F32)
        rfin[n] = value.astype(BF16)
        cols = pl.ds(pl.multiple_of(c * HALF, 128), HALF)
        for sub in range(2):
            src = rfin.at[n, pl.ds(sub * SUB, SUB)]
            dst = ret.at[n, :, cols]
            here = jnp.logical_and(own, yh == sub)

            @pl.when(here)
            def _():
                pltpu.make_async_copy(src, dst, r_ret.at[n, c]).start()

            copy = remote(src, dst, s_ret.at[n, sub], r_ret.at[n, c], dev(yh=sub, c=yh))

            @pl.when(jnp.logical_not(here))
            def _():
                copy.start()

            def done(here=here, copy=copy):
                @pl.when(jnp.logical_not(here))
                def _():
                    copy.wait_send()
            pending.append(done)

    def ret_wait(n):
        for h in range(2):
            dst = ret.at[n, :, h * HALF:(h + 1) * HALF]
            pltpu.make_async_copy(dst, dst, r_ret.at[n, h]).wait()

    def proj_part(r):
        both = jnp.concatenate([attb[0, r, :], attb[1, r, :]], axis=1)
        return dot(both, wo[...])

    def dmod_part(r):
        both = jnp.concatenate([dqb[0, r, :], dqb[1, r, :]], axis=1)
        return dot(both, wq[...], NT)

    def backward(key_slot, query_slot, valid, lse, delta, to_query, to_key, first=False):
        def block(t, carry):
            r = pl.ds(pl.multiple_of(t * 256, 256), 256)
            keys_ = ka[key_slot, r, :]
            query_ = qa[query_slot]
            grad_ = doa[query_slot]
            p = jnp.exp2(scores(keys_, query_) - lse) * valid
            d_prob = dot(va[key_slot, r, :], grad_, NT)
            ds = (p * (d_prob - delta)).astype(BF16)
            if to_query:
                dqt[...] += dot(keys_, ds, TN)
            if to_key:
                new_v = dot(p.astype(BF16), grad_)
                new_k = dot(ds, query_)
                if first:
                    dv[r, :] = new_v
                    dk[r, :] = new_k
                else:
                    dv[r, :] += new_v
                    dk[r, :] += new_k
            return carry
        lax.fori_loop(0, 3, block, 0)

    dqt[...] = jnp.zeros_like(dqt)
    arrived(attb.at[1 - c], r_core.at[4])
    rs_step(0, proj_part, 4)
    backward(slot, slot, one, lse, delta, True, True, True)
    rs_step(0, proj_part, 3)
    s_round(2)
    backward(slot_b, slot, key_tiles[1][1], lse, delta, True, False)
    rs_step(0, proj_part, 2)
    s_round(3)
    backward(slot_a, slot, key_tiles[2][1], lse, delta, True, False)
    rs_step(0, proj_part, 1)
    s_round(4)
    q_round(5)
    o_round(5)
    s_round(5)

    def from_stats(s, first):
        return jnp.concatenate([sta[s, first + i:first + i + 1, :] for i in range(6)], axis=1)

    s, valid = query_tiles[0]
    backward(slot, s, valid, from_stats(s, 0), from_stats(s, 8), False, True)
    rs_finish(0, proj_part)
    s, valid = query_tiles[1]
    backward(slot, s, valid, from_stats(s, 0), from_stats(s, 8), False, True)

    def through_norm(source, grad, row):
        r = lax.rsqrt(jnp.mean(source * source, axis=-1, keepdims=True) + EPS)
        g = grad * gains[row:row + 1, :]
        return r * g - source * (r * r * r) * jnp.mean(source * g, axis=-1, keepdims=True)

    dqt_rows = drecv
    dqt_rows[0] = dqt[...].T * FACTOR

    def norm_back(t, carry):
        r = pl.ds(pl.multiple_of(t * 256, 256), 256)
        rows = raw[r, :]
        dqb[c, r, :HD] = through_norm(rows[:, :HD], dqt_rows[0, r, :], 0).astype(BF16)
        dqb[c, r, HD:2 * HD] = through_norm(rows[:, HD:2 * HD], dk[r, :] * FACTOR, 1).astype(BF16)
        dqb[c, r, 2 * HD:] = dv[r, :].astype(BF16)
        return carry

    lax.fori_loop(0, 3, norm_back, 0)
    send(dqb.at[c], dqb.at[c], s_core.at[5], r_core.at[5], sibling)
    arrived(dqb.at[1 - c], r_core.at[5])
    rs_step(1, dmod_part, 4)
    rs_step(1, dmod_part, 3)
    rs_step(1, dmod_part, 2)
    rs_step(1, dmod_part, 1)

    ret_wait(0)
    res_out[...] = (hid[...].astype(F32) + gate * ret[0].astype(F32)).astype(BF16)
    rs_finish(1, dmod_part)
    hat, r = normed()
    ret_wait(1)
    g = ret[1].astype(F32) * (1.0 + scale)
    d_in = r * (g - jnp.mean(g, axis=-1, keepdims=True) - hat * jnp.mean(g * hat, axis=-1, keepdims=True))
    gh_out[...] = (cot[...].astype(F32) + d_in).astype(BF16)

    for done in pending:
        done()
    for t in range(3):
        r = pl.ds(t * 256, 256)
        remote(psend.at[r], precv.at[r], s_core.at[t], r_core.at[t], sibling).wait_send()


def per_device(hidden, cotangent, step_index, mod_table, w_qkv, qk_gains, w_out, tile_pairs, tile_owner):
    vm = pl.BlockSpec(memory_space=pltpu.VMEM)
    sm = pl.BlockSpec(memory_space=pltpu.SMEM)
    hbm = pl.BlockSpec(memory_space=pl.ANY)
    dma = pltpu.SemaphoreType.DMA
    mods = lax.dynamic_index_in_dim(mod_table, step_index[0], 0, keepdims=False)
    V = pltpu.VMEM
    return pl.pallas_call(
        kernel,
        out_shape=[jax.ShapeDtypeStruct(hidden.shape, BF16)] * 2,
        in_specs=[vm, vm, vm, hbm, vm, hbm, sm, sm],
        out_specs=[vm, vm],
        scratch_shapes=[
            V((SUB, D), BF16), V((SUB, D), BF16), V((TILE, HALF), BF16), V((TILE, HALF), BF16),
            V((HALF, 768), BF16), V((256, HALF), BF16), V((TILE, 384), F32), V((TILE, 384), F32), V((TILE, 384), F32),
            V((TILE, HD), F32), V((2, TILE, HD), F32),
            V((16, TILE, HD), BF16), V((16, TILE, HD), BF16), V((16, TILE, HD), BF16), V((16, TILE, HD), BF16),
            V((16, 16, HD), F32), V((2, TILE, HD), BF16), V((2, TILE, 384), BF16),
            V((HD, TILE), F32), V((HD, TILE), F32), V((TILE, HD), F32), V((TILE, HD), F32),
            V((2, 2, 336, HALF), BF16), V((2, 2, 336, HALF), BF16), V((2, CH, HALF), BF16), V((2, SUB, D), BF16),
            dma((2, 2)), dma((2, 2)), dma((2,)), dma((2,)), dma((2,)), dma((2, 8)), dma((2, 8)), dma((6,)), dma((6,)),
            dma((5, 20)), dma((5, 20)), dma((2, 8)), dma((2, 8)), dma((2, 2)), dma((2, 2)),
        ],
        compiler_params=pltpu.CompilerParams(
            collective_id=0, has_side_effects=True, vmem_limit_bytes=60 * 2 ** 20
        ),
        name="sublayer",
    )(
        hidden, cotangent, mods, w_qkv.reshape(D, 384),
        qk_gains, w_out.reshape(HD, D), tile_pairs, tile_owner,
    )


def solution(mesh):
    rows = P(("blk", "head"), None)
    in_specs = (
        rows, rows, P(), P(), P(None, "head", None), P(), P("head", None, None), P(), P(),
    )
    return jax.shard_map(
        per_device, mesh=mesh, in_specs=in_specs, out_specs=(rows, rows), check_vma=False
    )
```

```python
import functools

import jax
import jax.numpy as jnp
from jax import lax
from jax.experimental import pallas as pl
from jax.experimental.pallas import tpu as pltpu
from jax.sharding import PartitionSpec as P

EPS = 1e-6
TILE = 768
HD = 128
D = 3072
HALF = D // 2
SUB = 48
CH = 96
NZ = 8
F32 = jnp.float32
BF16 = jnp.bfloat16
FACTOR = HD ** -0.5
LOG2E = 1.4426950408889634
MESH = pl.DeviceIdType.MESH
NT = (((1,), (1,)), ((), ()))
TN = (((0,), (0,)), ((), ()))


def dot(a, b, dims=(((1,), (0,)), ((), ()))):
    return lax.dot_general(a, b, dims, preferred_element_type=F32)


def kernel(
    hid, cot, mods, wqkv, gains, wout, pairs, owner,
    res_out, gh_out,
    xs, cs, xg, cg, wq, wo, raw, psend, precv, dsend, drecv,
    qa, ka, va, doa, sta, attb, dqb, ot, dqt, dk, dv,
    rsnd, rrcv, rfin, ret, pbuf,
    s_cross, r_cross, s_w, r_w, l_w, s_z, r_z, s_core, r_core,
    s_pl, r_pl, s_rs, r_rs, s_ret, r_ret,
):
    head, blk = lax.axis_index("head"), lax.axis_index("blk")
    yh, z = head // 8, lax.rem(head, 8)
    x, yl, c = blk // 4, lax.rem(blk // 2, 2), lax.rem(blk, 2)
    y = yh * 2 + yl

    def dev(yh=yh, z=z, x=x, yl=yl, c=c):
        return (yh * 8 + z, (x * 2 + yl) * 2 + c)

    def at_y(yy):
        yy = lax.rem(yy + 4, 4)
        return dev(yh=yy // 2, yl=lax.rem(yy, 2))

    def at_x(xx):
        return dev(x=lax.rem(xx + 4, 4))

    def at_z(zz):
        return dev(z=lax.rem(zz + 8, 8))

    sibling = dev(c=1 - c)
    wpartner = dev(yh=1 - yh, yl=1 - yl)
    own = c == yh

    barrier = pltpu.get_barrier_semaphore()
    partners = [
        at_x(x + 1), at_x(x - 1), at_y(y + 1), at_y(y - 1), at_z(z + 1), at_z(z - 1),
        sibling, dev(yh=1 - yh), dev(yh=1 - yh, c=1 - c),
    ]
    for p in partners:
        pl.semaphore_signal(barrier, inc=1, device_id=p, device_id_type=MESH)

    shift = mods[0:1, :]
    scale = mods[1:2, :]
    gate = mods[2:3, :]

    def normed():
        rows = hid[...].astype(F32)
        center = rows - jnp.mean(rows, axis=-1, keepdims=True)
        spread = jnp.mean(center * center, axis=-1, keepdims=True)
        r = lax.rsqrt(spread + EPS)
        return center * r, r

    hat, _ = normed()
    xs[...] = (hat * (1.0 + scale) + shift).astype(BF16)
    cs[...] = (cot[...].astype(F32) * gate).astype(BF16)

    pl.semaphore_wait(barrier, len(partners))

    def remote(src, dst, ss, rs, target):
        return pltpu.make_async_remote_copy(
            src_ref=src, dst_ref=dst, send_sem=ss, recv_sem=rs,
            device_id=target, device_id_type=MESH,
        )

    pending = []

    def send(src, dst, ss, rs, target):
        copy = remote(src, dst, ss, rs, target)
        copy.start()
        pending.append(copy.wait_send)

    def arrived(dst, rs):
        remote(dst, dst, rs, rs, sibling).wait_recv()

    def rows_of(zz, sub, count=SUB):
        return pl.ds(pl.multiple_of(zz * CH + sub * SUB, 16), count)

    def cross_send(n, stage, grid):
        for h in range(2):
            src = stage.at[:, h * HALF:(h + 1) * HALF]
            dst = grid.at[rows_of(z, yh)]
            here = jnp.logical_and(own, c == h)

            @pl.when(here)
            def _():
                pltpu.make_async_copy(src, dst, r_cross.at[n, yh]).start()

            copy = remote(src, dst, s_cross.at[n, h], r_cross.at[n, yh], dev(yh=c, c=h))

            @pl.when(jnp.logical_not(here))
            def _():
                copy.start()

            def done(here=here, copy=copy):
                @pl.when(jnp.logical_not(here))
                def _():
                    copy.wait_send()
            pending.append(done)

    def cross_wait(n, grid):
        for sub in range(2):
            dst = grid.at[rows_of(z, sub)]
            pltpu.make_async_copy(dst, dst, r_cross.at[n, sub]).wait()

    cross_send(0, xs, xg)
    def lanes(first, size):
        return pl.ds(pl.multiple_of(first, 128), size)

    def rows16(first, size):
        return pl.ds(pl.multiple_of(first, 16), size)

    def w_view(n, hh, ox, part=None):
        q = lax.rem(x + ox + 4, 4) * 384
        if n == 0:
            size = 384 if part is None else 192
            return wq.at[rows16(q + (part or 0) * 192, size), lanes(hh * 384, 384)]
        size = HD if part is None else HD // 2
        return wo.at[rows16(hh * HD + (part or 0) * 64, size), lanes(q, 384)]

    w_moves = [(1, 0, None), (-1, 0, None), (1, -1, 0), (-1, 1, 1)]

    def w_start(n, *ids):
        for i in ids:
            sign, ox, part = w_moves[i]
            ref = w_view(n, 1 - yh, ox, part)
            send(ref, ref, s_w.at[n, i], r_w.at[n, i], at_x(x + sign))

    def w_wait(n, *ids):
        for i in ids:
            sign, ox, part = w_moves[i]
            arrived(w_view(n, 1 - yh, ox - sign, part), r_w.at[n, i])

    def w_quarter(n):
        arrived(w_view(n, 1 - yh, 0), r_w.at[n, 4])

    send(wqkv.at[rows16(c * HALF + x * 384, 384)], w_view(0, yh, 0), s_w.at[0, 4], r_w.at[0, 4], wpartner)
    wq_local = pltpu.make_async_copy(wqkv.at[rows16(c * HALF, HALF)], wq.at[:, lanes(yh * 384, 384)], l_w.at[0])
    wo_local = pltpu.make_async_copy(wout.at[:, lanes(c * HALF, HALF)], wo.at[rows16(yh * HD, HD)], l_w.at[1])
    wq_local.start()
    wo_local.start()
    cross_send(1, cs, cg)
    send(wout.at[:, lanes(c * HALF + x * 384, 384)], w_view(1, yh, 0), s_w.at[1, 4], r_w.at[1, 4], wpartner)

    def z_piece(grid, off, h):
        return grid.at[rows_of(lax.rem(z + off + 16, 8), h)]

    def z_step(n, grid, j):
        for h in range(2):
            for i, sign in enumerate((1, -1)):
                if j > 1:
                    arrived(z_piece(grid, -sign * (j - 1), h), r_z.at[n, (j - 2) * 4 + i * 2 + h])
                if j < 4 or h == i:
                    ref = z_piece(grid, -sign * (j - 1), h)
                    k = (j - 1) * 4 + i * 2 + h
                    send(ref, ref, s_z.at[n, k], r_z.at[n, k], at_z(z + sign))

    def z_end(n, grid):
        for i, sign in enumerate((1, -1)):
            arrived(z_piece(grid, -sign * 4, i), r_z.at[n, 12 + i * 3])

    cross_wait(0, xg)
    z_step(0, xg, 1)
    w_quarter(0)
    w_start(0, 0, 1)
    z_step(0, xg, 2)
    cross_wait(1, cg)
    w_quarter(1)
    w_start(1, 0, 1)
    z_step(0, xg, 3)
    w_wait(0, 0, 1)
    w_start(0, 2, 3)
    w_wait(1, 0, 1)
    w_start(1, 2, 3)
    z_step(0, xg, 4)
    z_step(1, cg, 1)
    w_wait(0, 2, 3)
    wq_local.wait()
    z_end(0, xg)

    def pick(first, second):
        return jnp.where(c == 0, first, second), jnp.where(c == 0, second, first)

    def qkv_rows(t, carry):
        r = pl.ds(pl.multiple_of(t * 256, 256), 256)
        part = dot(xg[r, :], wq[...])
        mine, other = pick(part[:, :384], part[:, 384:])
        raw[r, :] = mine
        psend[r, :] = other
        remote(psend.at[r], precv.at[r], s_core.at[t], r_core.at[t], sibling).start()
        return carry

    lax.fori_loop(0, 3, qkv_rows, 0)

    slot = x * 4 + y

    def rms(source, row):
        return lax.rsqrt(jnp.mean(source * source, axis=-1, keepdims=True) + EPS) * gains[row:row + 1, :]

    def norm_rows(t, carry):
        r = pl.ds(pl.multiple_of(t * 256, 256), 256)
        arrived(precv.at[r], r_core.at[t])
        total = raw[r, :] + precv[r, :]
        raw[r, :] = total
        query, key = total[:, :HD], total[:, HD:2 * HD]
        qa[slot, r, :] = (query * rms(query, 0)).astype(BF16)
        ka[slot, r, :] = (key * rms(key, 1)).astype(BF16)
        va[slot, r, :] = total[:, 2 * HD:].astype(BF16)
        return carry

    lax.fori_loop(0, 3, norm_rows, 0)

    def plane(n, ref, rows, swap):
        half = rows // 2

        def place(oa, ob):
            ox, oy = (ob, oa) if swap else (oa, ob)
            return lax.rem(x + ox + 4, 4) * 4 + lax.rem(y + oy + 4, 4)

        def target(axis, sign):
            on_x = (axis == 0) != swap
            return at_x(x + sign) if on_x else at_y(y + sign)

        moves = [(0, 1, 0, 0, None), (0, -1, 0, 0, None), (0, 1, -1, 0, 0), (0, -1, 1, 0, 1)]
        for oa in (0, -1, 1, -2):
            moves += [(1, 1, oa, 0, None), (1, -1, oa, 0, None), (1, 1, oa, -1, 0), (1, -1, oa, 1, 1)]

        def view(oa, ob, part):
            s = place(oa, ob)
            if part is None:
                return ref.at[s]
            return ref.at[s, pl.ds(part * half, half)]

        def start(*ids):
            for i in ids:
                axis, sign, oa, ob, part = moves[i]
                src = view(oa, ob, part)
                send(src, src, s_pl.at[n, i], r_pl.at[n, i], target(axis, sign))

        def wait(*ids):
            for i in ids:
                axis, sign, oa, ob, part = moves[i]
                if axis == 0:
                    oa = oa - sign
                else:
                    ob = ob - sign
                arrived(view(oa, ob, part), r_pl.at[n, i])

        def round_(k):
            if k == 1:
                start(0, 1, 4, 5)
            elif k == 2:
                wait(0, 1)
                start(2, 3, 8, 9, 12, 13)
                wait(4, 5)
                start(6, 7)
            elif k == 3:
                wait(2, 3)
                start(16, 17)
                wait(8, 9, 12, 13)
                start(10, 11, 14, 15)
            elif k == 4:
                wait(16, 17)
                start(18, 19)
            else:
                wait(6, 7, 10, 11, 14, 15, 18, 19)
        return round_

    k_round = plane(0, ka, TILE, False)
    v_round = plane(1, va, TILE, True)
    q_round = plane(2, qa, TILE, False)
    o_round = plane(3, doa, TILE, True)
    s_round = plane(4, sta, 16, False)

    k_round(1)
    v_round(1)
    z_step(1, cg, 2)
    k_round(2)
    v_round(2)
    z_step(1, cg, 3)
    z_step(1, cg, 4)
    w_wait(1, 2, 3)
    wo_local.wait()
    z_end(1, cg)

    def grad_rows(t, carry):
        r = pl.ds(pl.multiple_of(t * 256, 256), 256)
        part = dot(cg[r, :], wo[...], NT)
        mine, other = pick(part[:, :HD], part[:, HD:])
        drecv[0, r, :] = mine
        dsend[r, :] = other
        return carry

    lax.fori_loop(0, 3, grad_rows, 0)
    send(dsend, drecv.at[1], s_core.at[3], r_core.at[3], sibling)
    k_round(3)
    v_round(3)
    arrived(drecv.at[1], r_core.at[3])
    doa[slot] = (drecv[0] + drecv[1]).astype(BF16)

    def position(s):
        return (s // 4 * 2 + s % 2) * 2 + (s % 4) // 2

    tile = owner[(x * 2 + yl) * 2 + yh]
    before = lax.rem(tile + 15, 16)
    after = lax.rem(tile + 1, 16)
    slot_b = jnp.int32(0)
    slot_a = jnp.int32(0)
    for s in range(16):
        o = owner[position(s)]
        slot_b = jnp.where(o == before, s, slot_b)
        slot_a = jnp.where(o == after, s, slot_a)

    def lists(a, b):
        hit = jnp.float32(0.0)
        for n in range(3):
            hit = jnp.where(pairs[a, n] == b, 1.0, hit)
        return hit

    one = jnp.float32(1.0)
    key_tiles = [(slot, one), (slot_b, lists(tile, before)), (slot_a, lists(tile, after))]
    query_tiles = [(slot_b, lists(before, tile)), (slot_a, lists(after, tile))]
    EXPC = FACTOR * LOG2E

    def scores(keys_, query_):
        return dot(keys_, query_, NT) * EXPC

    ot[...] = jnp.zeros_like(ot)
    total = jnp.zeros((1, TILE), F32)

    def attend(total, entry):
        s, valid = entry

        def block(t, total):
            r = pl.ds(pl.multiple_of(t * 256, 256), 256)
            e = jnp.exp2(scores(ka[s, r, :], qa[slot])) * valid
            ot[...] += dot(va[s, r, :], e.astype(BF16), TN)
            return total + jnp.sum(e, axis=0, keepdims=True)
        return lax.fori_loop(0, 3, block, total)

    total = attend(total, key_tiles[0])
    k_round(4)
    v_round(4)
    q_round(1)
    o_round(1)
    k_round(5)
    v_round(5)
    total = attend(total, key_tiles[1])
    total = attend(total, key_tiles[2])
    out_t = (ot[...] / total).astype(BF16).astype(F32)
    attb[c] = out_t.T.astype(BF16)
    send(attb.at[c], attb.at[c], s_core.at[4], r_core.at[4], sibling)
    lse = jnp.log2(total)
    delta = jnp.sum(out_t * doa[slot].astype(F32).T, axis=0, keepdims=True)
    for i in range(6):
        sta[slot, i:i + 1, :] = lse[:, i * HD:(i + 1) * HD]
        sta[slot, 8 + i:9 + i, :] = delta[:, i * HD:(i + 1) * HD]
    s_round(1)

    base = {4: 0, 3: SUB, 2: SUB + CH, 1: SUB + 2 * CH}

    def rs_step(n, partial, j):
        if j == 4:
            pbuf[:CH, :] = partial([rows_of(lax.rem(z + 4, 8), 0, CH)])
        else:
            pbuf[...] = partial([rows_of(lax.rem(z + sign * j + 8, 8), 0, CH) for sign in (1, -1)])
        for h in range(2):
            for i, sign in enumerate((1, -1)):
                if j == 4 and h != i:
                    continue
                first = h * SUB + (0 if j == 4 else i * CH)
                value = pbuf[first:first + SUB, :]
                r = pl.ds(0 if j == 4 else base[j] + h * SUB, SUB)
                k = (j - 1) * 4 + i * 2 + h
                if j < 3 or (j == 3 and h == i):
                    prev = pl.ds(0 if j == 3 else base[j + 1] + h * SUB, SUB)
                    arrived(rrcv.at[n, i, prev], r_rs.at[n, k + 4])
                    value = value + rrcv[n, i, prev, :].astype(F32)
                rsnd[n, i, r, :] = value.astype(BF16)
                send(rsnd.at[n, i, r], rrcv.at[n, i, r], s_rs.at[n, k], r_rs.at[n, k], at_z(z + sign))

    def rs_finish(n, partial):
        pbuf[:CH, :] = partial([rows_of(z, 0, CH)])
        for h in range(2):
            value = pbuf[h * SUB:(h + 1) * SUB, :]
            r = pl.ds(base[1] + h * SUB, SUB)
            for i in range(2):
                arrived(rrcv.at[n, i, r], r_rs.at[n, i * 2 + h])
                value = value + rrcv[n, i, r, :].astype(F32)
            rfin[n, h * SUB:(h + 1) * SUB, :] = value.astype(BF16)
        cols = pl.ds(pl.multiple_of(c * HALF, 128), HALF)
        for sub in range(2):
            src = rfin.at[n, pl.ds(sub * SUB, SUB)]
            dst = ret.at[n, :, cols]
            here = jnp.logical_and(own, yh == sub)

            @pl.when(here)
            def _():
                pltpu.make_async_copy(src, dst, r_ret.at[n, c]).start()

            copy = remote(src, dst, s_ret.at[n, sub], r_ret.at[n, c], dev(yh=sub, c=yh))

            @pl.when(jnp.logical_not(here))
            def _():
                copy.start()

            def done(here=here, copy=copy):
                @pl.when(jnp.logical_not(here))
                def _():
                    copy.wait_send()
            pending.append(done)

    def ret_wait(n):
        for h in range(2):
            dst = ret.at[n, :, h * HALF:(h + 1) * HALF]
            pltpu.make_async_copy(dst, dst, r_ret.at[n, h]).wait()

    def stack(ref, spans):
        return jnp.concatenate(
            [jnp.concatenate([ref[0, r, :], ref[1, r, :]], axis=1) for r in spans], axis=0
        )

    def proj_part(spans):
        return dot(stack(attb, spans), wo[...])

    def dmod_part(spans):
        return dot(stack(dqb, spans), wq[...], NT)

    def backward(key_slot, query_slot, valid, lse, delta, to_query, to_key, first=False):
        def block(t, carry):
            r = pl.ds(pl.multiple_of(t * 256, 256), 256)
            keys_ = ka[key_slot, r, :]
            query_ = qa[query_slot]
            grad_ = doa[query_slot]
            p = jnp.exp2(scores(keys_, query_) - lse) * valid
            d_prob = dot(va[key_slot, r, :], grad_, NT)
            ds = (p * (d_prob - delta)).astype(BF16)
            if to_query:
                dqt[...] += dot(keys_, ds, TN)
            if to_key:
                new_v = dot(p.astype(BF16), grad_)
                new_k = dot(ds, query_)
                if first:
                    dv[r, :] = new_v
                    dk[r, :] = new_k
                else:
                    dv[r, :] += new_v
                    dk[r, :] += new_k
            return carry
        lax.fori_loop(0, 3, block, 0)

    dqt[...] = jnp.zeros_like(dqt)
    arrived(attb.at[1 - c], r_core.at[4])
    rs_step(0, proj_part, 4)
    q_round(2)
    o_round(2)
    s_round(2)
    backward(slot, slot, one, lse, delta, True, True, True)
    rs_step(0, proj_part, 3)
    backward(slot_b, slot, key_tiles[1][1], lse, delta, True, False)
    backward(slot_a, slot, key_tiles[2][1], lse, delta, True, False)
    rs_step(0, proj_part, 2)
    s_round(3)
    q_round(3)
    o_round(3)
    s_round(4)
    rs_step(0, proj_part, 1)
    q_round(4)
    o_round(4)
    rs_finish(0, proj_part)
    q_round(5)
    o_round(5)
    s_round(5)

    def from_stats(s, first):
        return jnp.concatenate([sta[s, first + i:first + i + 1, :] for i in range(6)], axis=1)

    s, valid = query_tiles[0]
    backward(slot, s, valid, from_stats(s, 0), from_stats(s, 8), False, True)
    s, valid = query_tiles[1]
    backward(slot, s, valid, from_stats(s, 0), from_stats(s, 8), False, True)

    def through_norm(source, grad, row):
        r = lax.rsqrt(jnp.mean(source * source, axis=-1, keepdims=True) + EPS)
        g = grad * gains[row:row + 1, :]
        return r * g - source * (r * r * r) * jnp.mean(source * g, axis=-1, keepdims=True)

    dqt_rows = drecv
    dqt_rows[0] = dqt[...].T * FACTOR

    def norm_back(t, carry):
        r = pl.ds(pl.multiple_of(t * 256, 256), 256)
        rows = raw[r, :]
        dqb[c, r, :HD] = through_norm(rows[:, :HD], dqt_rows[0, r, :], 0).astype(BF16)
        dqb[c, r, HD:2 * HD] = through_norm(rows[:, HD:2 * HD], dk[r, :] * FACTOR, 1).astype(BF16)
        dqb[c, r, 2 * HD:] = dv[r, :].astype(BF16)
        return carry

    lax.fori_loop(0, 3, norm_back, 0)
    send(dqb.at[c], dqb.at[c], s_core.at[5], r_core.at[5], sibling)
    arrived(dqb.at[1 - c], r_core.at[5])
    rs_step(1, dmod_part, 4)
    rs_step(1, dmod_part, 3)
    ret_wait(0)
    res_out[...] = (hid[...].astype(F32) + gate * ret[0].astype(F32)).astype(BF16)
    rs_step(1, dmod_part, 2)
    rs_step(1, dmod_part, 1)
    rs_finish(1, dmod_part)
    hat, r = normed()
    ret_wait(1)
    g = ret[1].astype(F32) * (1.0 + scale)
    d_in = r * (g - jnp.mean(g, axis=-1, keepdims=True) - hat * jnp.mean(g * hat, axis=-1, keepdims=True))
    gh_out[...] = (cot[...].astype(F32) + d_in).astype(BF16)

    for done in pending:
        done()
    for t in range(3):
        r = pl.ds(t * 256, 256)
        remote(psend.at[r], precv.at[r], s_core.at[t], r_core.at[t], sibling).wait_send()


def per_device(hidden, cotangent, step_index, mod_table, w_qkv, qk_gains, w_out, tile_pairs, tile_owner):
    vm = pl.BlockSpec(memory_space=pltpu.VMEM)
    sm = pl.BlockSpec(memory_space=pltpu.SMEM)
    hbm = pl.BlockSpec(memory_space=pl.ANY)
    dma = pltpu.SemaphoreType.DMA
    mods = lax.dynamic_index_in_dim(mod_table, step_index[0], 0, keepdims=False)
    V = pltpu.VMEM
    return pl.pallas_call(
        kernel,
        out_shape=[jax.ShapeDtypeStruct(hidden.shape, BF16)] * 2,
        in_specs=[vm, vm, vm, hbm, vm, hbm, sm, sm],
        out_specs=[vm, vm],
        scratch_shapes=[
            V((SUB, D), BF16), V((SUB, D), BF16), V((TILE, HALF), BF16), V((TILE, HALF), BF16),
            V((HALF, 768), BF16), V((256, HALF), BF16), V((TILE, 384), F32), V((TILE, 384), F32), V((TILE, 384), F32),
            V((TILE, HD), F32), V((2, TILE, HD), F32),
            V((16, TILE, HD), BF16), V((16, TILE, HD), BF16), V((16, TILE, HD), BF16), V((16, TILE, HD), BF16),
            V((16, 16, HD), F32), V((2, TILE, HD), BF16), V((2, TILE, 384), BF16),
            V((HD, TILE), F32), V((HD, TILE), F32), V((TILE, HD), F32), V((TILE, HD), F32),
            V((2, 2, 336, HALF), BF16), V((2, 2, 336, HALF), BF16), V((2, CH, HALF), BF16), V((2, SUB, D), BF16), V((2 * CH, HALF), F32),
            dma((2, 2)), dma((2, 2)), dma((2, 5)), dma((2, 5)), dma((2,)), dma((2, 16)), dma((2, 16)), dma((6,)), dma((6,)),
            dma((5, 20)), dma((5, 20)), dma((2, 16)), dma((2, 16)), dma((2, 2)), dma((2, 2)),
        ],
        compiler_params=pltpu.CompilerParams(
            collective_id=0, has_side_effects=True, vmem_limit_bytes=60 * 2 ** 20
        ),
        name="sublayer",
    )(
        hidden, cotangent, mods, w_qkv.reshape(D, 384),
        qk_gains, w_out.reshape(HD, D), tile_pairs, tile_owner,
    )


def solution(mesh):
    rows = P(("blk", "head"), None)
    in_specs = (
        rows, rows, P(), P(), P(None, "head", None), P(), P("head", None, None), P(), P(),
    )
    return jax.shard_map(
        per_device, mesh=mesh, in_specs=in_specs, out_specs=(rows, rows), check_vma=False
    )
```

```python
import functools

import jax
import jax.numpy as jnp
from jax import lax
from jax.experimental import pallas as pl
from jax.experimental.pallas import tpu as pltpu
from jax.sharding import PartitionSpec as P

EPS = 1e-6
TILE = 768
HALF_T = TILE // 2
HD = 128
D = 3072
HALF = D // 2
SUB = 48
CH = 96
NZ = 8
F32 = jnp.float32
BF16 = jnp.bfloat16
FACTOR = HD ** -0.5
LOG2E = 1.4426950408889634
MESH = pl.DeviceIdType.MESH
NT = (((1,), (1,)), ((), ()))
TN = (((0,), (0,)), ((), ()))


def dot(a, b, dims=(((1,), (0,)), ((), ()))):
    return lax.dot_general(a, b, dims, preferred_element_type=F32)


def kernel(
    hid, cot, mods, wqkv, gains, wout, pairs, owner,
    res_out, gh_out,
    xs, cs, xg, cg, wq, wo, raw, psend, precv, dsend, drecv,
    qa, ka, va, doa, sta, attb, dqb, ot, dqt, dk, dv,
    rsnd, rrcv, rfin, ret, pbuf,
    nk, nv, nq, no, gk, gv, gq, go_, near_s, far_s, inv,
    s_cross, r_cross, s_w, r_w, l_w, s_z, r_z, s_core, r_core,
    s_pl, r_pl, s_rs, r_rs, s_ret, r_ret,
):
    head, blk = lax.axis_index("head"), lax.axis_index("blk")
    yh, z = head // 8, lax.rem(head, 8)
    x, yl, c = blk // 4, lax.rem(blk // 2, 2), lax.rem(blk, 2)
    y = yh * 2 + yl

    def dev(yh=yh, z=z, x=x, yl=yl, c=c):
        return (yh * 8 + z, (x * 2 + yl) * 2 + c)

    def at_y(yy):
        yy = lax.rem(yy + 4, 4)
        return dev(yh=yy // 2, yl=lax.rem(yy, 2))

    def at_x(xx):
        return dev(x=lax.rem(xx + 4, 4))

    def at_z(zz):
        return dev(z=lax.rem(zz + 8, 8))

    sibling = dev(c=1 - c)
    wpartner = dev(yh=1 - yh, yl=1 - yl)
    own = c == yh

    barrier = pltpu.get_barrier_semaphore()
    partners = [
        at_x(x + 1), at_x(x - 1), at_y(y + 1), at_y(y - 1), at_z(z + 1), at_z(z - 1),
        sibling, dev(yh=1 - yh), dev(yh=1 - yh, c=1 - c),
    ]
    for p in partners:
        pl.semaphore_signal(barrier, inc=1, device_id=p, device_id_type=MESH)

    shift = mods[0:1, :]
    scale = mods[1:2, :]
    gate = mods[2:3, :]

    def normed():
        rows = hid[...].astype(F32)
        center = rows - jnp.mean(rows, axis=-1, keepdims=True)
        spread = jnp.mean(center * center, axis=-1, keepdims=True)
        r = lax.rsqrt(spread + EPS)
        return center * r, r

    hat, _ = normed()
    xs[...] = (hat * (1.0 + scale) + shift).astype(BF16)
    cs[...] = (cot[...].astype(F32) * gate).astype(BF16)

    owners = [owner[(s // 4 * 2 + s % 2) * 2 + (s % 4) // 2] for s in range(16)]
    for t in range(16):
        found = jnp.int32(0)
        for s in range(16):
            found = jnp.where(owners[s] == t, s, found)
        inv[t] = found

    pl.semaphore_wait(barrier, len(partners))

    def remote(src, dst, ss, rs, target):
        return pltpu.make_async_remote_copy(
            src_ref=src, dst_ref=dst, send_sem=ss, recv_sem=rs,
            device_id=target, device_id_type=MESH,
        )

    pending = []

    def send(src, dst, ss, rs, target):
        copy = remote(src, dst, ss, rs, target)
        copy.start()
        pending.append(copy.wait_send)

    def arrived(dst, rs):
        remote(dst, dst, rs, rs, sibling).wait_recv()

    def rows_of(zz, sub, count=SUB):
        return pl.ds(pl.multiple_of(zz * CH + sub * SUB, 16), count)

    def cross_send(n, stage, grid):
        for h in range(2):
            src = stage.at[:, h * HALF:(h + 1) * HALF]
            dst = grid.at[rows_of(z, yh)]
            here = jnp.logical_and(own, c == h)

            @pl.when(here)
            def _():
                pltpu.make_async_copy(src, dst, r_cross.at[n, yh]).start()

            copy = remote(src, dst, s_cross.at[n, h], r_cross.at[n, yh], dev(yh=c, c=h))

            @pl.when(jnp.logical_not(here))
            def _():
                copy.start()

            def done(here=here, copy=copy):
                @pl.when(jnp.logical_not(here))
                def _():
                    copy.wait_send()
            pending.append(done)

    def cross_wait(n, grid):
        for sub in range(2):
            dst = grid.at[rows_of(z, sub)]
            pltpu.make_async_copy(dst, dst, r_cross.at[n, sub]).wait()

    cross_send(0, xs, xg)
    def lanes(first, size):
        return pl.ds(pl.multiple_of(first, 128), size)

    def rows16(first, size):
        return pl.ds(pl.multiple_of(first, 16), size)

    def w_view(n, hh, ox, part=None):
        q = lax.rem(x + ox + 4, 4) * 384
        if n == 0:
            size = 384 if part is None else 192
            return wq.at[rows16(q + (part or 0) * 192, size), lanes(hh * 384, 384)]
        size = HD if part is None else HD // 2
        return wo.at[rows16(hh * HD + (part or 0) * 64, size), lanes(q, 384)]

    w_moves = [(1, 0, None), (-1, 0, None), (1, -1, 0), (-1, 1, 1)]

    def w_start(n, *ids):
        for i in ids:
            sign, ox, part = w_moves[i]
            ref = w_view(n, 1 - yh, ox, part)
            send(ref, ref, s_w.at[n, i], r_w.at[n, i], at_x(x + sign))

    def w_wait(n, *ids):
        for i in ids:
            sign, ox, part = w_moves[i]
            arrived(w_view(n, 1 - yh, ox - sign, part), r_w.at[n, i])

    def w_quarter(n):
        arrived(w_view(n, 1 - yh, 0), r_w.at[n, 4])

    wq_local = pltpu.make_async_copy(wqkv.at[rows16(c * HALF, HALF)], wq.at[:, lanes(yh * 384, 384)], l_w.at[0])
    wo_local = pltpu.make_async_copy(wout.at[:, lanes(c * HALF, HALF)], wo.at[rows16(yh * HD, HD)], l_w.at[1])
    wq_local.start()
    wo_local.start()

    def z_piece(grid, off, h):
        return grid.at[rows_of(lax.rem(z + off + 16, 8), h)]

    def z_step(n, grid, j):
        for h in range(2):
            for i, sign in enumerate((1, -1)):
                if j > 1:
                    arrived(z_piece(grid, -sign * (j - 1), h), r_z.at[n, (j - 2) * 4 + i * 2 + h])
                if j < 4 or h == i:
                    ref = z_piece(grid, -sign * (j - 1), h)
                    k = (j - 1) * 4 + i * 2 + h
                    send(ref, ref, s_z.at[n, k], r_z.at[n, k], at_z(z + sign))

    def z_end(n, grid):
        for i, sign in enumerate((1, -1)):
            arrived(z_piece(grid, -sign * 4, i), r_z.at[n, 12 + i * 3])

    cross_wait(0, xg)
    z_step(0, xg, 1)
    send(wqkv.at[rows16(c * HALF + x * 384, 384)], w_view(0, yh, 0), s_w.at[0, 4], r_w.at[0, 4], wpartner)
    cross_send(1, cs, cg)
    send(wout.at[:, lanes(c * HALF + x * 384, 384)], w_view(1, yh, 0), s_w.at[1, 4], r_w.at[1, 4], wpartner)
    w_quarter(0)
    w_start(0, 0, 1)
    z_step(0, xg, 2)
    cross_wait(1, cg)
    w_quarter(1)
    w_start(1, 0, 1)
    z_step(0, xg, 3)
    w_wait(0, 0, 1)
    w_start(0, 2, 3)
    w_wait(1, 0, 1)
    w_start(1, 2, 3)
    z_step(0, xg, 4)
    z_step(1, cg, 1)
    w_wait(0, 2, 3)
    wq_local.wait()
    z_end(0, xg)

    def pick(first, second):
        return jnp.where(c == 0, first, second), jnp.where(c == 0, second, first)

    def qkv_rows(t, carry):
        r = pl.ds(pl.multiple_of(t * 256, 256), 256)
        part = dot(xg[r, :], wq[...])
        mine, other = pick(part[:, :384], part[:, 384:])
        raw[r, :] = mine
        psend[r, :] = other
        remote(psend.at[r], precv.at[r], s_core.at[t], r_core.at[t], sibling).start()
        return carry

    lax.fori_loop(0, 3, qkv_rows, 0)

    slot = x * 4 + y

    def rms(source, row):
        return lax.rsqrt(jnp.mean(source * source, axis=-1, keepdims=True) + EPS) * gains[row:row + 1, :]

    def norm_rows(t, carry):
        r = pl.ds(pl.multiple_of(t * 256, 256), 256)
        arrived(precv.at[r], r_core.at[t])
        total = raw[r, :] + precv[r, :]
        raw[r, :] = total
        query, key = total[:, :HD], total[:, HD:2 * HD]
        qa[x, r, :] = (query * rms(query, 0)).astype(BF16)
        ka[x, r, :] = (key * rms(key, 1)).astype(BF16)
        va[y, r, :] = total[:, 2 * HD:].astype(BF16)
        return carry

    lax.fori_loop(0, 3, norm_rows, 0)

    def plane(n, ref, rows, swap):
        half = rows // 2

        def place(oa, ob):
            ox, oy = (ob, oa) if swap else (oa, ob)
            return lax.rem(x + ox + 4, 4) * 4 + lax.rem(y + oy + 4, 4)

        def target(axis, sign):
            on_x = (axis == 0) != swap
            return at_x(x + sign) if on_x else at_y(y + sign)

        moves = [(0, 1, 0, 0, None), (0, -1, 0, 0, None), (0, 1, -1, 0, 0), (0, -1, 1, 0, 1)]
        for oa in (0, -1, 1, -2):
            moves += [(1, 1, oa, 0, None), (1, -1, oa, 0, None), (1, 1, oa, -1, 0), (1, -1, oa, 1, 1)]

        def view(oa, ob, part):
            s = place(oa, ob)
            if part is None:
                return ref.at[s]
            return ref.at[s, pl.ds(part * half, half)]

        def start(*ids):
            for i in ids:
                axis, sign, oa, ob, part = moves[i]
                src = view(oa, ob, part)
                send(src, src, s_pl.at[n, i], r_pl.at[n, i], target(axis, sign))

        def wait(*ids):
            for i in ids:
                axis, sign, oa, ob, part = moves[i]
                if axis == 0:
                    oa = oa - sign
                else:
                    ob = ob - sign
                arrived(view(oa, ob, part), r_pl.at[n, i])

        def round_(k):
            if k == 1:
                start(0, 1, 4, 5)
            elif k == 2:
                wait(0, 1)
                start(2, 3, 8, 9, 12, 13)
                wait(4, 5)
                start(6, 7)
            elif k == 3:
                wait(2, 3)
                start(16, 17)
                wait(8, 9, 12, 13)
                start(10, 11, 14, 15)
            elif k == 4:
                wait(16, 17)
                start(18, 19)
            else:
                wait(6, 7, 10, 11, 14, 15, 18, 19)
        return round_

    FIRST, LAST = pl.ds(0, HALF_T), pl.ds(HALF_T, HALF_T)

    def neighbours(n, line, swap, mine, got, near, far):
        a, b = (y, x) if swap else (x, y)

        def target(axis, sign):
            on_x = (axis == 0) != swap
            return at_x(x + sign) if on_x else at_y(y + sign)

        def need(step, role):
            bb = lax.rem(b + step + 4, 4)
            xx, yy = (bb, a) if swap else (a, bb)
            tile = owner[(xx * 2 + lax.rem(yy, 2)) * 2 + yy // 2]
            s = inv[lax.rem(tile + (15 if role == 0 else 1), 16)]
            sx, sy = s // 4, lax.rem(s, 4)
            return (sy, sx) if swap else (sx, sy)

        def spot(off, part=None):
            ref = line.at[lax.rem(a + off + 4, 4)]
            return ref if part is None else ref.at[pl.ds(part * HALF_T, HALF_T)]

        def go(i, src, dst, axis, sign):
            send(src, dst, s_pl.at[n, i], r_pl.at[n, i], target(axis, sign))

        def has(i, dst):
            arrived(dst, r_pl.at[n, i])

        def round_(k):
            if k == 1:
                go(0, spot(0), spot(0), 0, 1)
                go(1, spot(0), spot(0), 0, -1)
            elif k == 2:
                has(0, spot(-1))
                go(2, spot(-1, 0), spot(-1, 0), 0, 1)
                has(1, spot(1))
                go(3, spot(1, 1), spot(1, 1), 0, -1)
            elif k == 3:
                has(2, spot(-2, 0))
                has(3, spot(2, 1))
                for role in range(2):
                    sa, _ = need(2, role)
                    for side in range(2):
                        far[0, role, side] = line[sa, pl.ds(side * HALF_T, HALF_T), :]
                        go(4 + role * 2 + side, far.at[0, role, side], far.at[1, role, side], 1, -1 if side == 0 else 1)
                for role in range(2):
                    sa, _ = need(-1, role)
                    near[0, role, LAST, :] = line[sa, LAST, :]
                    go(8 + role * 2, near.at[0, role, LAST], got.at[0, role, LAST], 1, -1)
                    sa, _ = need(1, role)
                    near[1, role, FIRST, :] = line[sa, FIRST, :]
                    go(9 + role * 2, near.at[1, role, FIRST], got.at[1, role, FIRST], 1, 1)
            elif k == 4:
                for role in range(2):
                    for side, part in ((0, FIRST), (1, LAST)):
                        sa, sb = need(-1 if side == 0 else 1, role)
                        has(4 + role * 2 + side, far.at[1, role, side])
                        near[side, role, part, :] = jnp.where(sb == b, line[sa, part, :], far[1, role, side])
                        go(12 + role * 2 + side, near.at[side, role, part], got.at[side, role, part], 1, -1 if side == 0 else 1)
            else:
                for role in range(2):
                    has(8 + role * 2, got.at[0, role, LAST])
                    has(9 + role * 2, got.at[1, role, FIRST])
                    has(12 + role * 2, got.at[0, role, FIRST])
                    has(13 + role * 2, got.at[1, role, LAST])
                for role in range(2):
                    sa, sb = need(0, role)
                    step = lax.rem(sb - b + 4, 4)
                    up = jnp.where(jnp.logical_or(step == 1, step == 2), 0, 1)
                    down = jnp.where(step >= 2, 1, 0)
                    mine[role, FIRST, :] = jnp.where(step == 0, line[sa, FIRST, :], got[up, role, FIRST, :])
                    mine[role, LAST, :] = jnp.where(step == 0, line[sa, LAST, :], got[down, role, LAST, :])
        return round_

    k_round = neighbours(0, ka, False, nk, gk, near_s.at[0], far_s.at[0])
    v_round = neighbours(1, va, True, nv, gv, near_s.at[1], far_s.at[1])
    q_round = neighbours(2, qa, False, nq, gq, near_s.at[2], far_s.at[2])
    o_round = neighbours(3, doa, True, no, go_, near_s.at[3], far_s.at[3])
    s_round = plane(4, sta, 16, False)

    tile = owner[(x * 2 + yl) * 2 + yh]
    before = lax.rem(tile + 15, 16)
    after = lax.rem(tile + 1, 16)
    slot_b = inv[before]
    slot_a = inv[after]

    def lists(a, b):
        hit = jnp.float32(0.0)
        for n in range(3):
            hit = jnp.where(pairs[a, n] == b, 1.0, hit)
        return hit

    one = jnp.float32(1.0)
    own_k, own_v, own_q, own_o = ka.at[x], va.at[y], qa.at[x], doa.at[y]
    key_tiles = [
        (own_k, own_v, one),
        (nk.at[0], nv.at[0], lists(tile, before)),
        (nk.at[1], nv.at[1], lists(tile, after)),
    ]
    query_tiles = [
        (nq.at[0], no.at[0], slot_b, lists(before, tile)),
        (nq.at[1], no.at[1], slot_a, lists(after, tile)),
    ]
    EXPC = FACTOR * LOG2E

    def scores(keys_, query_):
        return dot(keys_, query_, NT) * EXPC

    ot[...] = jnp.zeros_like(ot)
    total = jnp.zeros((1, TILE), F32)

    def attend(total, entry):
        keys_, values_, valid = entry

        def block(t, total):
            r = pl.ds(pl.multiple_of(t * 256, 256), 256)
            e = jnp.exp2(scores(keys_[r, :], own_q[...])) * valid
            ot[...] += dot(values_[r, :], e.astype(BF16), TN)
            return total + jnp.sum(e, axis=0, keepdims=True)
        return lax.fori_loop(0, 3, block, total)

    k_round(1)
    v_round(1)
    z_step(1, cg, 2)
    k_round(2)
    v_round(2)
    z_step(1, cg, 3)
    k_round(3)
    v_round(3)
    z_step(1, cg, 4)
    k_round(4)
    v_round(4)
    w_wait(1, 2, 3)
    wo_local.wait()
    z_end(1, cg)

    def grad_rows(t, carry):
        r = pl.ds(pl.multiple_of(t * 256, 256), 256)
        part = dot(cg[r, :], wo[...], NT)
        mine, other = pick(part[:, :HD], part[:, HD:])
        drecv[0, r, :] = mine
        dsend[r, :] = other
        return carry

    lax.fori_loop(0, 3, grad_rows, 0)
    send(dsend, drecv.at[1], s_core.at[3], r_core.at[3], sibling)
    total = attend(total, key_tiles[0])
    arrived(drecv.at[1], r_core.at[3])
    doa[y] = (drecv[0] + drecv[1]).astype(BF16)
    q_round(1)
    o_round(1)
    k_round(5)
    v_round(5)
    total = attend(total, key_tiles[1])
    total = attend(total, key_tiles[2])
    out_t = (ot[...] / total).astype(BF16).astype(F32)
    attb[c] = out_t.T.astype(BF16)
    send(attb.at[c], attb.at[c], s_core.at[4], r_core.at[4], sibling)
    lse = jnp.log2(total)
    delta = jnp.sum(out_t * own_o[...].astype(F32).T, axis=0, keepdims=True)
    for i in range(6):
        sta[slot, i:i + 1, :] = lse[:, i * HD:(i + 1) * HD]
        sta[slot, 8 + i:9 + i, :] = delta[:, i * HD:(i + 1) * HD]
    s_round(1)

    base = {4: 0, 3: SUB, 2: SUB + CH, 1: SUB + 2 * CH}

    def rs_step(n, partial, j):
        if j == 4:
            pbuf[:CH, :] = partial([rows_of(lax.rem(z + 4, 8), 0, CH)])
        else:
            pbuf[...] = partial([rows_of(lax.rem(z + sign * j + 8, 8), 0, CH) for sign in (1, -1)])
        for h in range(2):
            for i, sign in enumerate((1, -1)):
                if j == 4 and h != i:
                    continue
                first = h * SUB + (0 if j == 4 else i * CH)
                value = pbuf[first:first + SUB, :]
                r = pl.ds(0 if j == 4 else base[j] + h * SUB, SUB)
                k = (j - 1) * 4 + i * 2 + h
                if j < 3 or (j == 3 and h == i):
                    prev = pl.ds(0 if j == 3 else base[j + 1] + h * SUB, SUB)
                    arrived(rrcv.at[n, i, prev], r_rs.at[n, k + 4])
                    value = value + rrcv[n, i, prev, :].astype(F32)
                rsnd[n, i, r, :] = value.astype(BF16)
                send(rsnd.at[n, i, r], rrcv.at[n, i, r], s_rs.at[n, k], r_rs.at[n, k], at_z(z + sign))

    def rs_finish(n, partial):
        pbuf[:CH, :] = partial([rows_of(z, 0, CH)])
        for h in range(2):
            value = pbuf[h * SUB:(h + 1) * SUB, :]
            r = pl.ds(base[1] + h * SUB, SUB)
            for i in range(2):
                arrived(rrcv.at[n, i, r], r_rs.at[n, i * 2 + h])
                value = value + rrcv[n, i, r, :].astype(F32)
            rfin[n, h * SUB:(h + 1) * SUB, :] = value.astype(BF16)
        cols = pl.ds(pl.multiple_of(c * HALF, 128), HALF)
        for sub in range(2):
            src = rfin.at[n, pl.ds(sub * SUB, SUB)]
            dst = ret.at[n, :, cols]
            here = jnp.logical_and(own, yh == sub)

            @pl.when(here)
            def _():
                pltpu.make_async_copy(src, dst, r_ret.at[n, c]).start()

            copy = remote(src, dst, s_ret.at[n, sub], r_ret.at[n, c], dev(yh=sub, c=yh))

            @pl.when(jnp.logical_not(here))
            def _():
                copy.start()

            def done(here=here, copy=copy):
                @pl.when(jnp.logical_not(here))
                def _():
                    copy.wait_send()
            pending.append(done)

    def ret_wait(n):
        for h in range(2):
            dst = ret.at[n, :, h * HALF:(h + 1) * HALF]
            pltpu.make_async_copy(dst, dst, r_ret.at[n, h]).wait()

    def stack(ref, spans):
        return jnp.concatenate(
            [jnp.concatenate([ref[0, r, :], ref[1, r, :]], axis=1) for r in spans], axis=0
        )

    def proj_part(spans):
        return dot(stack(attb, spans), wo[...])

    def dmod_part(spans):
        return dot(stack(dqb, spans), wq[...], NT)

    def backward(kref, vref, qref, oref, valid, lse, delta, to_query, to_key, first=False):
        def block(t, carry):
            r = pl.ds(pl.multiple_of(t * 256, 256), 256)
            keys_ = kref[r, :]
            query_ = qref[...]
            grad_ = oref[...]
            p = jnp.exp2(scores(keys_, query_) - lse) * valid
            d_prob = dot(vref[r, :], grad_, NT)
            ds = (p * (d_prob - delta)).astype(BF16)
            if to_query:
                dqt[...] += dot(keys_, ds, TN)
            if to_key:
                new_v = dot(p.astype(BF16), grad_)
                new_k = dot(ds, query_)
                if first:
                    dv[r, :] = new_v
                    dk[r, :] = new_k
                else:
                    dv[r, :] += new_v
                    dk[r, :] += new_k
            return carry
        lax.fori_loop(0, 3, block, 0)

    dqt[...] = jnp.zeros_like(dqt)
    arrived(attb.at[1 - c], r_core.at[4])
    rs_step(0, proj_part, 4)
    q_round(2)
    o_round(2)
    q_round(3)
    o_round(3)
    s_round(2)
    rs_step(0, proj_part, 3)
    backward(own_k, own_v, own_q, own_o, one, lse, delta, True, True, True)
    s_round(3)
    rs_step(0, proj_part, 2)
    backward(nk.at[0], nv.at[0], own_q, own_o, key_tiles[1][2], lse, delta, True, False)
    q_round(4)
    o_round(4)
    s_round(4)
    backward(nk.at[1], nv.at[1], own_q, own_o, key_tiles[2][2], lse, delta, True, False)
    rs_step(0, proj_part, 1)
    q_round(5)
    o_round(5)
    s_round(5)

    def from_stats(s, first):
        return jnp.concatenate([sta[s, first + i:first + i + 1, :] for i in range(6)], axis=1)

    q_, o_, s, valid = query_tiles[0]
    backward(own_k, own_v, q_, o_, valid, from_stats(s, 0), from_stats(s, 8), False, True)
    q_, o_, s, valid = query_tiles[1]
    backward(own_k, own_v, q_, o_, valid, from_stats(s, 0), from_stats(s, 8), False, True)
    rs_finish(0, proj_part)

    def through_norm(source, grad, row):
        r = lax.rsqrt(jnp.mean(source * source, axis=-1, keepdims=True) + EPS)
        g = grad * gains[row:row + 1, :]
        return r * g - source * (r * r * r) * jnp.mean(source * g, axis=-1, keepdims=True)

    dqt_rows = drecv
    dqt_rows[0] = dqt[...].T * FACTOR

    def norm_back(t, carry):
        r = pl.ds(pl.multiple_of(t * 256, 256), 256)
        rows = raw[r, :]
        dqb[c, r, :HD] = through_norm(rows[:, :HD], dqt_rows[0, r, :], 0).astype(BF16)
        dqb[c, r, HD:2 * HD] = through_norm(rows[:, HD:2 * HD], dk[r, :] * FACTOR, 1).astype(BF16)
        dqb[c, r, 2 * HD:] = dv[r, :].astype(BF16)
        return carry

    lax.fori_loop(0, 3, norm_back, 0)
    send(dqb.at[c], dqb.at[c], s_core.at[5], r_core.at[5], sibling)
    arrived(dqb.at[1 - c], r_core.at[5])
    rs_step(1, dmod_part, 4)
    rs_step(1, dmod_part, 3)
    ret_wait(0)
    res_out[...] = (hid[...].astype(F32) + gate * ret[0].astype(F32)).astype(BF16)
    rs_step(1, dmod_part, 2)
    rs_step(1, dmod_part, 1)
    rs_finish(1, dmod_part)
    hat, r = normed()
    ret_wait(1)
    g = ret[1].astype(F32) * (1.0 + scale)
    d_in = r * (g - jnp.mean(g, axis=-1, keepdims=True) - hat * jnp.mean(g * hat, axis=-1, keepdims=True))
    gh_out[...] = (cot[...].astype(F32) + d_in).astype(BF16)

    for done in pending:
        done()
    for t in range(3):
        r = pl.ds(t * 256, 256)
        remote(psend.at[r], precv.at[r], s_core.at[t], r_core.at[t], sibling).wait_send()


def per_device(hidden, cotangent, step_index, mod_table, w_qkv, qk_gains, w_out, tile_pairs, tile_owner):
    vm = pl.BlockSpec(memory_space=pltpu.VMEM)
    sm = pl.BlockSpec(memory_space=pltpu.SMEM)
    hbm = pl.BlockSpec(memory_space=pl.ANY)
    dma = pltpu.SemaphoreType.DMA
    mods = lax.dynamic_index_in_dim(mod_table, step_index[0], 0, keepdims=False)
    V = pltpu.VMEM
    return pl.pallas_call(
        kernel,
        out_shape=[jax.ShapeDtypeStruct(hidden.shape, BF16)] * 2,
        in_specs=[vm, vm, vm, hbm, vm, hbm, sm, sm],
        out_specs=[vm, vm],
        scratch_shapes=[
            V((SUB, D), BF16), V((SUB, D), BF16), V((TILE, HALF), BF16), V((TILE, HALF), BF16),
            V((HALF, 768), BF16), V((256, HALF), BF16), V((TILE, 384), F32), V((TILE, 384), F32), V((TILE, 384), F32),
            V((TILE, HD), F32), V((2, TILE, HD), F32),
            *[V((4, TILE, HD), BF16)] * 4,
            V((16, 16, HD), F32), V((2, TILE, HD), BF16), V((2, TILE, 384), BF16),
            V((HD, TILE), F32), V((HD, TILE), F32), V((TILE, HD), F32), V((TILE, HD), F32),
            V((2, 2, 336, HALF), BF16), V((2, 2, 336, HALF), BF16), V((2, CH, HALF), BF16), V((2, SUB, D), BF16), V((2 * CH, HALF), F32),
            *[V((2, TILE, HD), BF16)] * 4, *[V((2, 2, TILE, HD), BF16)] * 4,
            V((4, 2, 2, TILE, HD), BF16), V((4, 2, 2, 2, HALF_T, HD), BF16), pltpu.SMEM((16,), jnp.int32),
            dma((2, 2)), dma((2, 2)), dma((2, 5)), dma((2, 5)), dma((2,)), dma((2, 16)), dma((2, 16)), dma((6,)), dma((6,)),
            dma((5, 20)), dma((5, 20)), dma((2, 16)), dma((2, 16)), dma((2, 2)), dma((2, 2)),
        ],
        compiler_params=pltpu.CompilerParams(
            collective_id=0, has_side_effects=True, vmem_limit_bytes=60 * 2 ** 20
        ),
        name="sublayer",
    )(
        hidden, cotangent, mods, w_qkv.reshape(D, 384),
        qk_gains, w_out.reshape(HD, D), tile_pairs, tile_owner,
    )


def solution(mesh):
    rows = P(("blk", "head"), None)
    in_specs = (
        rows, rows, P(), P(), P(None, "head", None), P(), P("head", None, None), P(), P(),
    )
    return jax.shard_map(
        per_device, mesh=mesh, in_specs=in_specs, out_specs=(rows, rows), check_vma=False
    )
```

```python
import functools

import jax
import jax.numpy as jnp
from jax import lax
from jax.experimental import pallas as pl
from jax.experimental.pallas import tpu as pltpu
from jax.sharding import PartitionSpec as P

EPS = 1e-6
TILE = 768
HALF_T = TILE // 2
HD = 128
D = 3072
HALF = D // 2
SUB = 48
CH = 96
NZ = 8
F32 = jnp.float32
BF16 = jnp.bfloat16
FACTOR = HD ** -0.5
LOG2E = 1.4426950408889634
MESH = pl.DeviceIdType.MESH
NT = (((1,), (1,)), ((), ()))
TN = (((0,), (0,)), ((), ()))


def dot(a, b, dims=(((1,), (0,)), ((), ()))):
    return lax.dot_general(a, b, dims, preferred_element_type=F32)


def kernel(
    hid, cot, step_ref, modt, wqkv, gains, wout, pairs, owner,
    res_out, gh_out,
    xs, cs, xg, cg, wq, wo, raw, psend, precv, dsend, drecv,
    qa, ka, va, doa, sta, attb, dqb, ot, dqt, dk, dv,
    rsnd, rrcv, rfin, ret, pbuf,
    nk, nv, nq, no, gk, gv, gq, go_, near_s, far_s, inv,
    s_cross, r_cross, s_w, r_w, l_w, s_z, r_z, s_core, r_core,
    s_pl, r_pl, s_rs, r_rs, s_ret, r_ret,
):
    head, blk = lax.axis_index("head"), lax.axis_index("blk")
    yh, z = head // 8, lax.rem(head, 8)
    x, yl, c = blk // 4, lax.rem(blk // 2, 2), lax.rem(blk, 2)
    y = yh * 2 + yl

    def dev(yh=yh, z=z, x=x, yl=yl, c=c):
        return (yh * 8 + z, (x * 2 + yl) * 2 + c)

    def at_y(yy):
        yy = lax.rem(yy + 4, 4)
        return dev(yh=yy // 2, yl=lax.rem(yy, 2))

    def at_x(xx):
        return dev(x=lax.rem(xx + 4, 4))

    def at_z(zz):
        return dev(z=lax.rem(zz + 8, 8))

    sibling = dev(c=1 - c)
    wpartner = dev(yh=1 - yh, yl=1 - yl)
    own = c == yh

    barrier = pltpu.get_barrier_semaphore()
    partners = [
        at_x(x + 1), at_x(x - 1), at_y(y + 1), at_y(y - 1), at_z(z + 1), at_z(z - 1),
        sibling, dev(yh=1 - yh), dev(yh=1 - yh, c=1 - c),
    ]
    for p in partners:
        pl.semaphore_signal(barrier, inc=1, device_id=p, device_id_type=MESH)

    step = step_ref[0]
    shift = modt[0, pl.ds(step, 1), :]
    scale = modt[1, pl.ds(step, 1), :]
    gate = modt[2, pl.ds(step, 1), :]

    def normed():
        rows = hid[...].astype(F32)
        center = rows - jnp.mean(rows, axis=-1, keepdims=True)
        spread = jnp.mean(center * center, axis=-1, keepdims=True)
        r = lax.rsqrt(spread + EPS)
        return center * r, r

    hat, _ = normed()
    xs[...] = (hat * (1.0 + scale) + shift).astype(BF16)
    cs[...] = (cot[...].astype(F32) * gate).astype(BF16)

    owners = [owner[(s // 4 * 2 + s % 2) * 2 + (s % 4) // 2] for s in range(16)]
    for t in range(16):
        found = jnp.int32(0)
        for s in range(16):
            found = jnp.where(owners[s] == t, s, found)
        inv[t] = found

    pl.semaphore_wait(barrier, len(partners))

    def remote(src, dst, ss, rs, target):
        return pltpu.make_async_remote_copy(
            src_ref=src, dst_ref=dst, send_sem=ss, recv_sem=rs,
            device_id=target, device_id_type=MESH,
        )

    pending = []

    def send(src, dst, ss, rs, target):
        copy = remote(src, dst, ss, rs, target)
        copy.start()
        pending.append(copy.wait_send)

    def arrived(dst, rs):
        remote(dst, dst, rs, rs, sibling).wait_recv()

    def rows_of(zz, sub, count=SUB):
        return pl.ds(pl.multiple_of(zz * CH + sub * SUB, 16), count)

    def cross_send(n, stage, grid):
        for h in range(2):
            src = stage.at[:, h * HALF:(h + 1) * HALF]
            dst = grid.at[rows_of(z, yh)]
            here = jnp.logical_and(own, c == h)

            @pl.when(here)
            def _():
                pltpu.make_async_copy(src, dst, r_cross.at[n, yh]).start()

            copy = remote(src, dst, s_cross.at[n, h], r_cross.at[n, yh], dev(yh=c, c=h))

            @pl.when(jnp.logical_not(here))
            def _():
                copy.start()

            def done(here=here, copy=copy):
                @pl.when(jnp.logical_not(here))
                def _():
                    copy.wait_send()
            pending.append(done)

    def cross_wait(n, grid, sub):
        dst = grid.at[rows_of(z, sub)]
        pltpu.make_async_copy(dst, dst, r_cross.at[n, sub]).wait()

    cross_send(0, xs, xg)

    def lanes(first, size):
        return pl.ds(pl.multiple_of(first, 128), size)

    def rows16(first, size):
        return pl.ds(pl.multiple_of(first, 16), size)

    def w_view(n, hh, ox, part=None):
        q = lax.rem(x + ox + 4, 4) * 384
        if n == 0:
            size = 384 if part is None else 192
            return wq.at[rows16(q + (part or 0) * 192, size), lanes(hh * 384, 384)]
        size = HD if part is None else HD // 2
        return wo.at[rows16(hh * HD + (part or 0) * 64, size), lanes(q, 384)]

    w_moves = [(1, 0, None), (-1, 0, None), (1, -1, 0), (-1, 1, 1)]

    def w_start(n, *ids):
        for i in ids:
            sign, ox, part = w_moves[i]
            ref = w_view(n, 1 - yh, ox, part)
            send(ref, ref, s_w.at[n, i], r_w.at[n, i], at_x(x + sign))

    def w_wait(n, *ids):
        for i in ids:
            sign, ox, part = w_moves[i]
            arrived(w_view(n, 1 - yh, ox - sign, part), r_w.at[n, i])

    def w_quarter(n):
        arrived(w_view(n, 1 - yh, 0), r_w.at[n, 4])

    wq_local = pltpu.make_async_copy(wqkv.at[rows16(c * HALF, HALF)], wq.at[:, lanes(yh * 384, 384)], l_w.at[0])
    wo_local = pltpu.make_async_copy(wout.at[:, lanes(c * HALF, HALF)], wo.at[rows16(yh * HD, HD)], l_w.at[1])
    wq_local.start()
    wo_local.start()

    def z_piece(grid, off, h):
        return grid.at[rows_of(lax.rem(z + off + 16, 8), h)]

    def z_step(n, grid, j):
        for h in (yh, 1 - yh) if j < 4 else (0, 1):
            if j == 1:
                cross_wait(n, grid, h)
            for i, sign in enumerate((1, -1)):
                if j > 1:
                    arrived(z_piece(grid, -sign * (j - 1), h), r_z.at[n, (j - 2) * 4 + i * 2 + h])
                if j < 4 or h == i:
                    ref = z_piece(grid, -sign * (j - 1), h)
                    k = (j - 1) * 4 + i * 2 + h
                    send(ref, ref, s_z.at[n, k], r_z.at[n, k], at_z(z + sign))

    def z_end(n, grid):
        for i, sign in enumerate((1, -1)):
            arrived(z_piece(grid, -sign * 4, i), r_z.at[n, 12 + i * 3])

    z_step(0, xg, 1)
    send(wqkv.at[rows16(c * HALF + x * 384, 384)], w_view(0, yh, 0), s_w.at[0, 4], r_w.at[0, 4], wpartner)
    cross_send(1, cs, cg)
    send(wout.at[:, lanes(c * HALF + x * 384, 384)], w_view(1, yh, 0), s_w.at[1, 4], r_w.at[1, 4], wpartner)
    z_step(0, xg, 2)
    w_quarter(0)
    w_start(0, 0, 1)
    z_step(0, xg, 3)
    w_quarter(1)
    w_start(1, 0, 1)
    w_wait(0, 0, 1)
    w_start(0, 2, 3)
    z_step(0, xg, 4)
    z_step(1, cg, 1)
    w_wait(1, 0, 1)
    w_start(1, 2, 3)
    w_wait(0, 2, 3)
    wq_local.wait()
    z_end(0, xg)

    def pick(first, second):
        return jnp.where(c == 0, first, second), jnp.where(c == 0, second, first)

    def qkv_rows(t, carry):
        r = pl.ds(pl.multiple_of(t * 256, 256), 256)
        part = dot(xg[r, :], wq[...])
        mine, other = pick(part[:, :384], part[:, 384:])
        raw[r, :] = mine
        psend[r, :] = other
        remote(psend.at[r], precv.at[r], s_core.at[t], r_core.at[t], sibling).start()
        return carry

    lax.fori_loop(0, 3, qkv_rows, 0)

    slot = x * 4 + y

    def rms(source, row):
        return lax.rsqrt(jnp.mean(source * source, axis=-1, keepdims=True) + EPS) * gains[row:row + 1, :]

    def norm_rows(t, carry):
        r = pl.ds(pl.multiple_of(t * 256, 256), 256)
        arrived(precv.at[r], r_core.at[t])
        total = raw[r, :] + precv[r, :]
        raw[r, :] = total
        query, key = total[:, :HD], total[:, HD:2 * HD]
        qa[x, r, :] = (query * rms(query, 0)).astype(BF16)
        ka[x, r, :] = (key * rms(key, 1)).astype(BF16)
        va[y, r, :] = total[:, 2 * HD:].astype(BF16)
        return carry

    lax.fori_loop(0, 3, norm_rows, 0)

    def plane(n, ref, rows, swap):
        half = rows // 2

        def place(oa, ob):
            ox, oy = (ob, oa) if swap else (oa, ob)
            return lax.rem(x + ox + 4, 4) * 4 + lax.rem(y + oy + 4, 4)

        def target(axis, sign):
            on_x = (axis == 0) != swap
            return at_x(x + sign) if on_x else at_y(y + sign)

        moves = [(0, 1, 0, 0, None), (0, -1, 0, 0, None), (0, 1, -1, 0, 0), (0, -1, 1, 0, 1)]
        for oa in (0, -1, 1, -2):
            moves += [(1, 1, oa, 0, None), (1, -1, oa, 0, None), (1, 1, oa, -1, 0), (1, -1, oa, 1, 1)]

        def view(oa, ob, part):
            s = place(oa, ob)
            if part is None:
                return ref.at[s]
            return ref.at[s, pl.ds(part * half, half)]

        def start(*ids):
            for i in ids:
                axis, sign, oa, ob, part = moves[i]
                src = view(oa, ob, part)
                send(src, src, s_pl.at[n, i], r_pl.at[n, i], target(axis, sign))

        def wait(*ids):
            for i in ids:
                axis, sign, oa, ob, part = moves[i]
                if axis == 0:
                    oa = oa - sign
                else:
                    ob = ob - sign
                arrived(view(oa, ob, part), r_pl.at[n, i])

        def round_(k):
            if k == 1:
                start(0, 1, 4, 5)
            elif k == 2:
                wait(0, 1)
                start(2, 3, 8, 9, 12, 13)
                wait(4, 5)
                start(6, 7)
            elif k == 3:
                wait(2, 3)
                start(16, 17)
                wait(8, 9, 12, 13)
                start(10, 11, 14, 15)
            elif k == 4:
                wait(16, 17)
                start(18, 19)
            else:
                wait(6, 7, 10, 11, 14, 15, 18, 19)
        return round_

    FIRST, LAST = pl.ds(0, HALF_T), pl.ds(HALF_T, HALF_T)

    def neighbours(n, line, swap, mine, got, near, far):
        a, b = (y, x) if swap else (x, y)

        def target(axis, sign):
            on_x = (axis == 0) != swap
            return at_x(x + sign) if on_x else at_y(y + sign)

        def need(step, role):
            bb = lax.rem(b + step + 4, 4)
            xx, yy = (bb, a) if swap else (a, bb)
            tile = owner[(xx * 2 + lax.rem(yy, 2)) * 2 + yy // 2]
            s = inv[lax.rem(tile + (15 if role == 0 else 1), 16)]
            sx, sy = s // 4, lax.rem(s, 4)
            return (sy, sx) if swap else (sx, sy)

        def spot(off, part=None):
            ref = line.at[lax.rem(a + off + 4, 4)]
            return ref if part is None else ref.at[pl.ds(part * HALF_T, HALF_T)]

        def go(i, src, dst, axis, sign):
            send(src, dst, s_pl.at[n, i], r_pl.at[n, i], target(axis, sign))

        def has(i, dst):
            arrived(dst, r_pl.at[n, i])

        def round_(k):
            if k == 1:
                go(0, spot(0), spot(0), 0, 1)
                go(1, spot(0), spot(0), 0, -1)
            elif k == 2:
                has(0, spot(-1))
                go(2, spot(-1, 0), spot(-1, 0), 0, 1)
                has(1, spot(1))
                go(3, spot(1, 1), spot(1, 1), 0, -1)
            elif k == 3:
                has(2, spot(-2, 0))
                has(3, spot(2, 1))
                for role in range(2):
                    sa, _ = need(2, role)
                    for side in range(2):
                        far[0, role, side] = line[sa, pl.ds(side * HALF_T, HALF_T), :]
                        go(4 + role * 2 + side, far.at[0, role, side], far.at[1, role, side], 1, -1 if side == 0 else 1)
                for role in range(2):
                    sa, _ = need(-1, role)
                    near[0, role, LAST, :] = line[sa, LAST, :]
                    go(8 + role * 2, near.at[0, role, LAST], got.at[0, role, LAST], 1, -1)
                    sa, _ = need(1, role)
                    near[1, role, FIRST, :] = line[sa, FIRST, :]
                    go(9 + role * 2, near.at[1, role, FIRST], got.at[1, role, FIRST], 1, 1)
            elif k == 4:
                for role in range(2):
                    for side, part in ((0, FIRST), (1, LAST)):
                        sa, sb = need(-1 if side == 0 else 1, role)
                        has(4 + role * 2 + side, far.at[1, role, side])
                        near[side, role, part, :] = jnp.where(sb == b, line[sa, part, :], far[1, role, side])
                        go(12 + role * 2 + side, near.at[side, role, part], got.at[side, role, part], 1, -1 if side == 0 else 1)
            else:
                for role in range(2):
                    has(8 + role * 2, got.at[0, role, LAST])
                    has(9 + role * 2, got.at[1, role, FIRST])
                    has(12 + role * 2, got.at[0, role, FIRST])
                    has(13 + role * 2, got.at[1, role, LAST])
                for role in range(2):
                    sa, sb = need(0, role)
                    step = lax.rem(sb - b + 4, 4)
                    up = jnp.where(jnp.logical_or(step == 1, step == 2), 0, 1)
                    down = jnp.where(step >= 2, 1, 0)
                    mine[role, FIRST, :] = jnp.where(step == 0, line[sa, FIRST, :], got[up, role, FIRST, :])
                    mine[role, LAST, :] = jnp.where(step == 0, line[sa, LAST, :], got[down, role, LAST, :])
        return round_

    k_round = neighbours(0, ka, False, nk, gk, near_s.at[0], far_s.at[0])
    v_round = neighbours(1, va, True, nv, gv, near_s.at[1], far_s.at[1])
    q_round = neighbours(2, qa, False, nq, gq, near_s.at[2], far_s.at[2])
    o_round = neighbours(3, doa, True, no, go_, near_s.at[3], far_s.at[3])
    s_round = plane(4, sta, 16, False)

    tile = owner[(x * 2 + yl) * 2 + yh]
    before = lax.rem(tile + 15, 16)
    after = lax.rem(tile + 1, 16)
    slot_b = inv[before]
    slot_a = inv[after]

    def lists(a, b):
        hit = jnp.float32(0.0)
        for n in range(3):
            hit = jnp.where(pairs[n, a] == b, 1.0, hit)
        return hit

    one = jnp.float32(1.0)
    own_k, own_v, own_q, own_o = ka.at[x], va.at[y], qa.at[x], doa.at[y]
    key_tiles = [
        (own_k, own_v, one),
        (nk.at[0], nv.at[0], lists(tile, before)),
        (nk.at[1], nv.at[1], lists(tile, after)),
    ]
    query_tiles = [
        (nq.at[0], no.at[0], slot_b, lists(before, tile)),
        (nq.at[1], no.at[1], slot_a, lists(after, tile)),
    ]
    EXPC = FACTOR * LOG2E

    def scores(keys_, query_):
        return dot(keys_, query_, NT) * EXPC

    ot[...] = jnp.zeros_like(ot)
    total = jnp.zeros((1, TILE), F32)

    def attend(total, entry):
        keys_, values_, valid = entry

        def block(t, total):
            r = pl.ds(pl.multiple_of(t * 256, 256), 256)
            e = jnp.exp2(scores(keys_[r, :], own_q[...])) * valid
            ot[...] += dot(values_[r, :], e.astype(BF16), TN)
            return total + jnp.sum(e, axis=0, keepdims=True)
        return lax.fori_loop(0, 3, block, total)

    k_round(1)
    v_round(1)
    z_step(1, cg, 2)
    k_round(2)
    v_round(2)
    z_step(1, cg, 3)
    k_round(3)
    v_round(3)
    z_step(1, cg, 4)
    k_round(4)
    v_round(4)
    w_wait(1, 2, 3)
    wo_local.wait()
    z_end(1, cg)

    def grad_rows(t, carry):
        r = pl.ds(pl.multiple_of(t * 256, 256), 256)
        part = dot(cg[r, :], wo[...], NT)
        mine, other = pick(part[:, :HD], part[:, HD:])
        drecv[0, r, :] = mine
        dsend[r, :] = other
        return carry

    lax.fori_loop(0, 3, grad_rows, 0)
    send(dsend, drecv.at[1], s_core.at[3], r_core.at[3], sibling)
    total = attend(total, key_tiles[0])
    arrived(drecv.at[1], r_core.at[3])
    doa[y] = (drecv[0] + drecv[1]).astype(BF16)
    q_round(1)
    o_round(1)
    k_round(5)
    v_round(5)
    total = attend(total, key_tiles[1])
    total = attend(total, key_tiles[2])
    out_t = (ot[...] / total).astype(BF16).astype(F32)
    attb[c] = out_t.T.astype(BF16)
    send(attb.at[c], attb.at[c], s_core.at[4], r_core.at[4], sibling)
    lse = jnp.log2(total)
    delta = jnp.sum(out_t * own_o[...].astype(F32).T, axis=0, keepdims=True)
    for i in range(6):
        sta[slot, i:i + 1, :] = lse[:, i * HD:(i + 1) * HD]
        sta[slot, 8 + i:9 + i, :] = delta[:, i * HD:(i + 1) * HD]
    s_round(1)

    base = {4: 0, 3: SUB, 2: SUB + CH, 1: SUB + 2 * CH}

    def rs_step(n, partial, j):
        if j == 4:
            pbuf[:CH, :] = partial([rows_of(lax.rem(z + 4, 8), 0, CH)])
        else:
            pbuf[...] = partial([rows_of(lax.rem(z + sign * j + 8, 8), 0, CH) for sign in (1, -1)])
        for h in range(2):
            for i, sign in enumerate((1, -1)):
                if j == 4 and h != i:
                    continue
                first = h * SUB + (0 if j == 4 else i * CH)
                value = pbuf[first:first + SUB, :]
                r = pl.ds(0 if j == 4 else base[j] + h * SUB, SUB)
                k = (j - 1) * 4 + i * 2 + h
                if j < 3 or (j == 3 and h == i):
                    prev = pl.ds(0 if j == 3 else base[j + 1] + h * SUB, SUB)
                    arrived(rrcv.at[n, i, prev], r_rs.at[n, k + 4])
                    value = value + rrcv[n, i, prev, :].astype(F32)
                rsnd[n, i, r, :] = value.astype(BF16)
                send(rsnd.at[n, i, r], rrcv.at[n, i, r], s_rs.at[n, k], r_rs.at[n, k], at_z(z + sign))

    def rs_finish(n, partial):
        pbuf[:CH, :] = partial([rows_of(z, 0, CH)])
        for h in range(2):
            value = pbuf[h * SUB:(h + 1) * SUB, :]
            r = pl.ds(base[1] + h * SUB, SUB)
            for i in range(2):
                arrived(rrcv.at[n, i, r], r_rs.at[n, i * 2 + h])
                value = value + rrcv[n, i, r, :].astype(F32)
            rfin[n, h * SUB:(h + 1) * SUB, :] = value.astype(BF16)
        cols = pl.ds(pl.multiple_of(c * HALF, 128), HALF)
        for sub in range(2):
            src = rfin.at[n, pl.ds(sub * SUB, SUB)]
            dst = ret.at[n, :, cols]
            here = jnp.logical_and(own, yh == sub)

            @pl.when(here)
            def _():
                pltpu.make_async_copy(src, dst, r_ret.at[n, c]).start()

            copy = remote(src, dst, s_ret.at[n, sub], r_ret.at[n, c], dev(yh=sub, c=yh))

            @pl.when(jnp.logical_not(here))
            def _():
                copy.start()

            def done(here=here, copy=copy):
                @pl.when(jnp.logical_not(here))
                def _():
                    copy.wait_send()
            pending.append(done)

    def ret_wait(n):
        for h in range(2):
            dst = ret.at[n, :, h * HALF:(h + 1) * HALF]
            pltpu.make_async_copy(dst, dst, r_ret.at[n, h]).wait()

    def stack(ref, spans):
        return jnp.concatenate(
            [jnp.concatenate([ref[0, r, :], ref[1, r, :]], axis=1) for r in spans], axis=0
        )

    def proj_part(spans):
        return dot(stack(attb, spans), wo[...])

    def dmod_part(spans):
        return dot(stack(dqb, spans), wq[...], NT)

    def backward(kref, vref, qref, oref, valid, lse, delta, to_query, to_key, first=False):
        def block(t, carry):
            r = pl.ds(pl.multiple_of(t * 256, 256), 256)
            keys_ = kref[r, :]
            query_ = qref[...]
            grad_ = oref[...]
            p = jnp.exp2(scores(keys_, query_) - lse) * valid
            d_prob = dot(vref[r, :], grad_, NT)
            ds = (p * (d_prob - delta)).astype(BF16)
            if to_query:
                dqt[...] += dot(keys_, ds, TN)
            if to_key:
                new_v = dot(p.astype(BF16), grad_)
                new_k = dot(ds, query_)
                if first:
                    dv[r, :] = new_v
                    dk[r, :] = new_k
                else:
                    dv[r, :] += new_v
                    dk[r, :] += new_k
            return carry
        lax.fori_loop(0, 3, block, 0)

    dqt[...] = jnp.zeros_like(dqt)
    arrived(attb.at[1 - c], r_core.at[4])
    rs_step(0, proj_part, 4)
    q_round(2)
    o_round(2)
    q_round(3)
    o_round(3)
    s_round(2)
    rs_step(0, proj_part, 3)
    backward(own_k, own_v, own_q, own_o, one, lse, delta, True, True, True)
    s_round(3)
    rs_step(0, proj_part, 2)
    backward(nk.at[0], nv.at[0], own_q, own_o, key_tiles[1][2], lse, delta, True, False)
    q_round(4)
    o_round(4)
    s_round(4)
    backward(nk.at[1], nv.at[1], own_q, own_o, key_tiles[2][2], lse, delta, True, False)
    rs_step(0, proj_part, 1)
    q_round(5)
    o_round(5)
    s_round(5)

    def from_stats(s, first):
        return jnp.concatenate([sta[s, first + i:first + i + 1, :] for i in range(6)], axis=1)

    q_, o_, s, valid = query_tiles[0]
    backward(own_k, own_v, q_, o_, valid, from_stats(s, 0), from_stats(s, 8), False, True)
    q_, o_, s, valid = query_tiles[1]
    backward(own_k, own_v, q_, o_, valid, from_stats(s, 0), from_stats(s, 8), False, True)
    rs_finish(0, proj_part)

    def through_norm(source, grad, row):
        r = lax.rsqrt(jnp.mean(source * source, axis=-1, keepdims=True) + EPS)
        g = grad * gains[row:row + 1, :]
        return r * g - source * (r * r * r) * jnp.mean(source * g, axis=-1, keepdims=True)

    dqt_rows = drecv
    dqt_rows[0] = dqt[...].T * FACTOR

    def norm_back(t, carry):
        r = pl.ds(pl.multiple_of(t * 256, 256), 256)
        rows = raw[r, :]
        dqb[c, r, :HD] = through_norm(rows[:, :HD], dqt_rows[0, r, :], 0).astype(BF16)
        dqb[c, r, HD:2 * HD] = through_norm(rows[:, HD:2 * HD], dk[r, :] * FACTOR, 1).astype(BF16)
        dqb[c, r, 2 * HD:] = dv[r, :].astype(BF16)
        return carry

    lax.fori_loop(0, 3, norm_back, 0)
    send(dqb.at[c], dqb.at[c], s_core.at[5], r_core.at[5], sibling)
    arrived(dqb.at[1 - c], r_core.at[5])
    rs_step(1, dmod_part, 4)
    rs_step(1, dmod_part, 3)
    ret_wait(0)
    res_out[...] = (hid[...].astype(F32) + gate * ret[0].astype(F32)).astype(BF16)
    rs_step(1, dmod_part, 2)
    rs_step(1, dmod_part, 1)
    rs_finish(1, dmod_part)
    hat, r = normed()
    ret_wait(1)
    g = ret[1].astype(F32) * (1.0 + scale)
    d_in = r * (g - jnp.mean(g, axis=-1, keepdims=True) - hat * jnp.mean(g * hat, axis=-1, keepdims=True))
    gh_out[...] = (cot[...].astype(F32) + d_in).astype(BF16)

    for done in pending:
        done()
    for t in range(3):
        r = pl.ds(t * 256, 256)
        remote(psend.at[r], precv.at[r], s_core.at[t], r_core.at[t], sibling).wait_send()


def per_device(hidden, cotangent, step_index, mod_table, w_qkv, qk_gains, w_out, tile_pairs, tile_owner):
    vm = pl.BlockSpec(memory_space=pltpu.VMEM)
    sm = pl.BlockSpec(memory_space=pltpu.SMEM)
    hbm = pl.BlockSpec(memory_space=pl.ANY)
    dma = pltpu.SemaphoreType.DMA
    V = pltpu.VMEM
    return pl.pallas_call(
        kernel,
        out_shape=[jax.ShapeDtypeStruct(hidden.shape, BF16)] * 2,
        in_specs=[vm, vm, sm, vm, hbm, vm, hbm, sm, sm],
        out_specs=[vm, vm],
        scratch_shapes=[
            V((SUB, D), BF16), V((SUB, D), BF16), V((TILE, HALF), BF16), V((TILE, HALF), BF16),
            V((HALF, 768), BF16), V((256, HALF), BF16), V((TILE, 384), F32), V((TILE, 384), F32), V((TILE, 384), F32),
            V((TILE, HD), F32), V((2, TILE, HD), F32),
            *[V((4, TILE, HD), BF16)] * 4,
            V((16, 16, HD), F32), V((2, TILE, HD), BF16), V((2, TILE, 384), BF16),
            V((HD, TILE), F32), V((HD, TILE), F32), V((TILE, HD), F32), V((TILE, HD), F32),
            V((2, 2, 336, HALF), BF16), V((2, 2, 336, HALF), BF16), V((2, CH, HALF), BF16), V((2, SUB, D), BF16), V((2 * CH, HALF), F32),
            *[V((2, TILE, HD), BF16)] * 4, *[V((2, 2, TILE, HD), BF16)] * 4,
            V((4, 2, 2, TILE, HD), BF16), V((4, 2, 2, 2, HALF_T, HD), BF16), pltpu.SMEM((16,), jnp.int32),
            dma((2, 2)), dma((2, 2)), dma((2, 5)), dma((2, 5)), dma((2,)), dma((2, 16)), dma((2, 16)), dma((6,)), dma((6,)),
            dma((5, 20)), dma((5, 20)), dma((2, 16)), dma((2, 16)), dma((2, 2)), dma((2, 2)),
        ],
        compiler_params=pltpu.CompilerParams(
            collective_id=0, has_side_effects=True, vmem_limit_bytes=60 * 2 ** 20
        ),
        name="sublayer",
    )(
        hidden, cotangent, step_index, jnp.transpose(mod_table, (1, 0, 2)), w_qkv.reshape(D, 384),
        qk_gains, w_out.reshape(HD, D), tile_pairs.T, tile_owner,
    )


def solution(mesh):
    rows = P(("blk", "head"), None)
    in_specs = (
        rows, rows, P(), P(), P(None, "head", None), P(), P("head", None, None), P(), P(),
    )
    return jax.shard_map(
        per_device, mesh=mesh, in_specs=in_specs, out_specs=(rows, rows), check_vma=False
    )
```

```python
import functools

import jax
import jax.numpy as jnp
from jax import lax
from jax.experimental import pallas as pl
from jax.experimental.pallas import tpu as pltpu
from jax.sharding import PartitionSpec as P

EPS = 1e-6
TILE = 768
HALF_T = TILE // 2
HD = 128
D = 3072
HALF = D // 2
SUB = 48
CH = 96
NZ = 8
F32 = jnp.float32
BF16 = jnp.bfloat16
FACTOR = HD ** -0.5
LOG2E = 1.4426950408889634
MESH = pl.DeviceIdType.MESH
NT = (((1,), (1,)), ((), ()))
TN = (((0,), (0,)), ((), ()))


def dot(a, b, dims=(((1,), (0,)), ((), ()))):
    return lax.dot_general(a, b, dims, preferred_element_type=F32)


def kernel(
    hid, cot, step_ref, modt, wqkv, gains, wout, pairs, owner,
    res_out, gh_out,
    xs, cs, xg, cg, wq, wo, raw, psend, precv, dsend, drecv,
    qa, ka, va, doa, sta, attb, dqb, ot, dqt, dk, dv,
    rsnd, rrcv, rfin, ret, pbuf,
    nk, nv, nq, no, gk, gv, gq, go_, near_s, far_s, inv,
    s_cross, r_cross, s_w, r_w, l_w, s_z, r_z, s_core, r_core,
    s_pl, r_pl, s_rs, r_rs, s_ret, r_ret,
):
    head, blk = lax.axis_index("head"), lax.axis_index("blk")
    yh, z = head // 8, lax.rem(head, 8)
    x, yl, c = blk // 4, lax.rem(blk // 2, 2), lax.rem(blk, 2)
    y = yh * 2 + yl

    def dev(yh=yh, z=z, x=x, yl=yl, c=c):
        return (yh * 8 + z, (x * 2 + yl) * 2 + c)

    def at_y(yy):
        yy = lax.rem(yy + 4, 4)
        return dev(yh=yy // 2, yl=lax.rem(yy, 2))

    def at_x(xx):
        return dev(x=lax.rem(xx + 4, 4))

    def at_z(zz):
        return dev(z=lax.rem(zz + 8, 8))

    sibling = dev(c=1 - c)
    wpartner = dev(yh=1 - yh, yl=1 - yl)
    own = c == yh

    barrier = pltpu.get_barrier_semaphore()
    partners = [
        at_x(x + 1), at_x(x - 1), at_y(y + 1), at_y(y - 1), at_z(z + 1), at_z(z - 1),
        sibling, dev(yh=1 - yh), dev(yh=1 - yh, c=1 - c),
    ]
    for p in partners:
        pl.semaphore_signal(barrier, inc=1, device_id=p, device_id_type=MESH)

    step = step_ref[0]
    shift = modt[0, pl.ds(step, 1), :]
    scale = modt[1, pl.ds(step, 1), :]
    gate = modt[2, pl.ds(step, 1), :]

    def normed():
        rows = hid[...].astype(F32)
        center = rows - jnp.mean(rows, axis=-1, keepdims=True)
        spread = jnp.mean(center * center, axis=-1, keepdims=True)
        r = lax.rsqrt(spread + EPS)
        return center * r, r

    hat, _ = normed()
    xs[...] = (hat * (1.0 + scale) + shift).astype(BF16)
    cs[...] = (cot[...].astype(F32) * gate).astype(BF16)

    owners = [owner[(s // 4 * 2 + s % 2) * 2 + (s % 4) // 2] for s in range(16)]
    for t in range(16):
        found = jnp.int32(0)
        for s in range(16):
            found = jnp.where(owners[s] == t, s, found)
        inv[t] = found

    pl.semaphore_wait(barrier, len(partners))

    def remote(src, dst, ss, rs, target):
        return pltpu.make_async_remote_copy(
            src_ref=src, dst_ref=dst, send_sem=ss, recv_sem=rs,
            device_id=target, device_id_type=MESH,
        )

    pending = []

    def send(src, dst, ss, rs, target):
        copy = remote(src, dst, ss, rs, target)
        copy.start()
        pending.append(copy.wait_send)

    def arrived(dst, rs):
        remote(dst, dst, rs, rs, sibling).wait_recv()

    def rows_of(zz, sub, count=SUB):
        return pl.ds(pl.multiple_of(zz * CH + sub * SUB, 16), count)

    def cross_send(n, stage, grid):
        for h in range(2):
            src = stage.at[:, h * HALF:(h + 1) * HALF]
            dst = grid.at[rows_of(z, yh)]
            here = jnp.logical_and(own, c == h)

            @pl.when(here)
            def _():
                pltpu.make_async_copy(src, dst, r_cross.at[n, yh]).start()

            copy = remote(src, dst, s_cross.at[n, h], r_cross.at[n, yh], dev(yh=c, c=h))

            @pl.when(jnp.logical_not(here))
            def _():
                copy.start()

            def done(here=here, copy=copy):
                @pl.when(jnp.logical_not(here))
                def _():
                    copy.wait_send()
            pending.append(done)

    def cross_wait(n, grid, sub):
        dst = grid.at[rows_of(z, sub)]
        pltpu.make_async_copy(dst, dst, r_cross.at[n, sub]).wait()

    cross_send(0, xs, xg)

    def lanes(first, size):
        return pl.ds(pl.multiple_of(first, 128), size)

    def rows16(first, size):
        return pl.ds(pl.multiple_of(first, 16), size)

    def w_view(n, hh, ox, part=None):
        q = lax.rem(x + ox + 4, 4) * 384
        if n == 0:
            size = 384 if part is None else 192
            return wq.at[rows16(q + (part or 0) * 192, size), lanes(hh * 384, 384)]
        size = HD if part is None else HD // 2
        return wo.at[rows16(hh * HD + (part or 0) * 64, size), lanes(q, 384)]

    w_moves = [(1, 0, None), (-1, 0, None), (1, -1, 0), (-1, 1, 1)]

    def w_start(n, *ids):
        for i in ids:
            sign, ox, part = w_moves[i]
            ref = w_view(n, 1 - yh, ox, part)
            send(ref, ref, s_w.at[n, i], r_w.at[n, i], at_x(x + sign))

    def w_wait(n, *ids):
        for i in ids:
            sign, ox, part = w_moves[i]
            arrived(w_view(n, 1 - yh, ox - sign, part), r_w.at[n, i])

    def w_quarter(n):
        arrived(w_view(n, 1 - yh, 0), r_w.at[n, 4])

    wq_local = pltpu.make_async_copy(wqkv.at[rows16(c * HALF, HALF)], wq.at[:, lanes(yh * 384, 384)], l_w.at[0])
    wo_local = pltpu.make_async_copy(wout.at[:, lanes(c * HALF, HALF)], wo.at[rows16(yh * HD, HD)], l_w.at[1])
    wq_local.start()
    wo_local.start()

    def z_piece(grid, off, h):
        return grid.at[rows_of(lax.rem(z + off + 16, 8), h)]

    def z_step(n, grid, j):
        for h in (yh, 1 - yh) if j < 4 else (0, 1):
            if j == 1:
                cross_wait(n, grid, h)
            for i, sign in enumerate((1, -1)):
                if j > 1:
                    arrived(z_piece(grid, -sign * (j - 1), h), r_z.at[n, (j - 2) * 4 + i * 2 + h])
                if j < 4 or h == i:
                    ref = z_piece(grid, -sign * (j - 1), h)
                    k = (j - 1) * 4 + i * 2 + h
                    send(ref, ref, s_z.at[n, k], r_z.at[n, k], at_z(z + sign))

    def z_end(n, grid):
        for i, sign in enumerate((1, -1)):
            arrived(z_piece(grid, -sign * 4, i), r_z.at[n, 12 + i * 3])

    z_step(0, xg, 1)
    send(wqkv.at[rows16(c * HALF + x * 384, 384)], w_view(0, yh, 0), s_w.at[0, 4], r_w.at[0, 4], wpartner)
    cross_send(1, cs, cg)
    send(wout.at[:, lanes(c * HALF + x * 384, 384)], w_view(1, yh, 0), s_w.at[1, 4], r_w.at[1, 4], wpartner)
    z_step(0, xg, 2)
    w_quarter(0)
    w_start(0, 0, 1)
    z_step(0, xg, 3)
    w_quarter(1)
    w_start(1, 0, 1)
    w_wait(0, 0, 1)
    w_start(0, 2, 3)
    z_step(0, xg, 4)
    z_step(1, cg, 1)
    w_wait(1, 0, 1)
    w_start(1, 2, 3)
    w_wait(0, 2, 3)
    wq_local.wait()
    z_end(0, xg)

    def pick(first, second):
        return jnp.where(c == 0, first, second), jnp.where(c == 0, second, first)

    def qkv_rows(t, carry):
        r = pl.ds(pl.multiple_of(t * 256, 256), 256)
        part = dot(xg[r, :], wq[...])
        mine, other = pick(part[:, :384], part[:, 384:])
        raw[r, :] = mine
        psend[r, :] = other
        remote(psend.at[r], precv.at[r], s_core.at[t], r_core.at[t], sibling).start()
        return carry

    lax.fori_loop(0, 3, qkv_rows, 0)

    slot = x * 4 + y

    def rms(source, row):
        return lax.rsqrt(jnp.mean(source * source, axis=-1, keepdims=True) + EPS) * gains[row:row + 1, :]

    def norm_rows(t, carry):
        r = pl.ds(pl.multiple_of(t * 256, 256), 256)
        arrived(precv.at[r], r_core.at[t])
        total = raw[r, :] + precv[r, :]
        raw[r, :] = total
        query, key = total[:, :HD], total[:, HD:2 * HD]
        qa[x, r, :] = (query * rms(query, 0)).astype(BF16)
        ka[x, r, :] = (key * rms(key, 1)).astype(BF16)
        va[y, r, :] = total[:, 2 * HD:].astype(BF16)
        return carry

    lax.fori_loop(0, 3, norm_rows, 0)

    def plane(n, ref, rows, swap):
        half = rows // 2

        def place(oa, ob):
            ox, oy = (ob, oa) if swap else (oa, ob)
            return lax.rem(x + ox + 4, 4) * 4 + lax.rem(y + oy + 4, 4)

        def target(axis, sign):
            on_x = (axis == 0) != swap
            return at_x(x + sign) if on_x else at_y(y + sign)

        moves = [(0, 1, 0, 0, None), (0, -1, 0, 0, None), (0, 1, -1, 0, 0), (0, -1, 1, 0, 1)]
        for oa in (0, -1, 1, -2):
            moves += [(1, 1, oa, 0, None), (1, -1, oa, 0, None), (1, 1, oa, -1, 0), (1, -1, oa, 1, 1)]

        def view(oa, ob, part):
            s = place(oa, ob)
            if part is None:
                return ref.at[s]
            return ref.at[s, pl.ds(part * half, half)]

        def start(*ids):
            for i in ids:
                axis, sign, oa, ob, part = moves[i]
                src = view(oa, ob, part)
                send(src, src, s_pl.at[n, i], r_pl.at[n, i], target(axis, sign))

        def wait(*ids):
            for i in ids:
                axis, sign, oa, ob, part = moves[i]
                if axis == 0:
                    oa = oa - sign
                else:
                    ob = ob - sign
                arrived(view(oa, ob, part), r_pl.at[n, i])

        def round_(k):
            if k == 1:
                start(0, 1, 4, 5)
            elif k == 2:
                wait(0, 1)
                start(2, 3, 8, 9, 12, 13)
                wait(4, 5)
                start(6, 7)
            elif k == 3:
                wait(2, 3)
                start(16, 17)
                wait(8, 9, 12, 13)
                start(10, 11, 14, 15)
            elif k == 4:
                wait(16, 17)
                start(18, 19)
            else:
                wait(6, 7, 10, 11, 14, 15, 18, 19)
        return round_

    FIRST, LAST = pl.ds(0, HALF_T), pl.ds(HALF_T, HALF_T)

    def neighbours(n, line, swap, mine, got, near, far):
        a, b = (y, x) if swap else (x, y)

        def target(axis, sign):
            on_x = (axis == 0) != swap
            return at_x(x + sign) if on_x else at_y(y + sign)

        def need(step, role):
            bb = lax.rem(b + step + 4, 4)
            xx, yy = (bb, a) if swap else (a, bb)
            tile = owner[(xx * 2 + lax.rem(yy, 2)) * 2 + yy // 2]
            s = inv[lax.rem(tile + (15 if role == 0 else 1), 16)]
            sx, sy = s // 4, lax.rem(s, 4)
            return (sy, sx) if swap else (sx, sy)

        def spot(off, part=None):
            ref = line.at[lax.rem(a + off + 4, 4)]
            return ref if part is None else ref.at[pl.ds(part * HALF_T, HALF_T)]

        def go(i, src, dst, axis, sign):
            send(src, dst, s_pl.at[n, i], r_pl.at[n, i], target(axis, sign))

        def has(i, dst):
            arrived(dst, r_pl.at[n, i])

        def round_(k):
            if k == 1:
                go(0, spot(0), spot(0), 0, 1)
                go(1, spot(0), spot(0), 0, -1)
            elif k == 2:
                has(0, spot(-1))
                go(2, spot(-1, 0), spot(-1, 0), 0, 1)
                has(1, spot(1))
                go(3, spot(1, 1), spot(1, 1), 0, -1)
            elif k == 3:
                has(2, spot(-2, 0))
                has(3, spot(2, 1))
                for role in range(2):
                    sa, _ = need(2, role)
                    for side in range(2):
                        far[0, role, side] = line[sa, pl.ds(side * HALF_T, HALF_T), :]
                        go(4 + role * 2 + side, far.at[0, role, side], far.at[1, role, side], 1, -1 if side == 0 else 1)
                for role in range(2):
                    sa, _ = need(-1, role)
                    near[0, role, LAST, :] = line[sa, LAST, :]
                    go(8 + role * 2, near.at[0, role, LAST], got.at[0, role, LAST], 1, -1)
                    sa, _ = need(1, role)
                    near[1, role, FIRST, :] = line[sa, FIRST, :]
                    go(9 + role * 2, near.at[1, role, FIRST], got.at[1, role, FIRST], 1, 1)
            elif k == 4:
                for role in range(2):
                    for side, part in ((0, FIRST), (1, LAST)):
                        sa, sb = need(-1 if side == 0 else 1, role)
                        has(4 + role * 2 + side, far.at[1, role, side])
                        near[side, role, part, :] = jnp.where(sb == b, line[sa, part, :], far[1, role, side])
                        go(12 + role * 2 + side, near.at[side, role, part], got.at[side, role, part], 1, -1 if side == 0 else 1)
            else:
                for role in range(2):
                    has(8 + role * 2, got.at[0, role, LAST])
                    has(9 + role * 2, got.at[1, role, FIRST])
                    has(12 + role * 2, got.at[0, role, FIRST])
                    has(13 + role * 2, got.at[1, role, LAST])
                for role in range(2):
                    sa, sb = need(0, role)
                    step = lax.rem(sb - b + 4, 4)
                    up = jnp.where(jnp.logical_or(step == 1, step == 2), 0, 1)
                    down = jnp.where(step >= 2, 1, 0)
                    mine[role, FIRST, :] = jnp.where(step == 0, line[sa, FIRST, :], got[up, role, FIRST, :])
                    mine[role, LAST, :] = jnp.where(step == 0, line[sa, LAST, :], got[down, role, LAST, :])
        return round_

    k_round = neighbours(0, ka, False, nk, gk, near_s.at[0], far_s.at[0])
    v_round = neighbours(1, va, True, nv, gv, near_s.at[1], far_s.at[1])
    q_round = neighbours(2, qa, False, nq, gq, near_s.at[2], far_s.at[2])
    o_round = neighbours(3, doa, True, no, go_, near_s.at[3], far_s.at[3])
    s_round = plane(4, sta, 16, False)

    tile = owner[(x * 2 + yl) * 2 + yh]
    before = lax.rem(tile + 15, 16)
    after = lax.rem(tile + 1, 16)
    slot_b = inv[before]
    slot_a = inv[after]

    def lists(a, b):
        hit = jnp.float32(0.0)
        for n in range(3):
            hit = jnp.where(pairs[n, a] == b, 1.0, hit)
        return hit

    one = jnp.float32(1.0)
    own_k, own_v, own_q, own_o = ka.at[x], va.at[y], qa.at[x], doa.at[y]
    key_tiles = [
        (own_k, own_v, one),
        (nk.at[0], nv.at[0], lists(tile, before)),
        (nk.at[1], nv.at[1], lists(tile, after)),
    ]
    query_tiles = [
        (nq.at[0], no.at[0], slot_b, lists(before, tile)),
        (nq.at[1], no.at[1], slot_a, lists(after, tile)),
    ]
    EXPC = FACTOR * LOG2E

    def scores(keys_, query_):
        return dot(keys_, query_, NT) * EXPC

    ot[...] = jnp.zeros_like(ot)
    total = jnp.zeros((1, TILE), F32)

    def attend(total, entry):
        keys_, values_, valid = entry

        def block(t, total):
            r = pl.ds(pl.multiple_of(t * 256, 256), 256)
            e = jnp.exp2(scores(keys_[r, :], own_q[...])) * valid
            ot[...] += dot(values_[r, :], e.astype(BF16), TN)
            return total + jnp.sum(e, axis=0, keepdims=True)
        return lax.fori_loop(0, 3, block, total)

    k_round(1)
    v_round(1)
    z_step(1, cg, 2)
    k_round(2)
    v_round(2)
    z_step(1, cg, 3)
    k_round(3)
    v_round(3)
    z_step(1, cg, 4)
    k_round(4)
    v_round(4)
    w_wait(1, 2, 3)
    wo_local.wait()
    z_end(1, cg)

    def grad_rows(t, carry):
        r = pl.ds(pl.multiple_of(t * 256, 256), 256)
        part = dot(cg[r, :], wo[...], NT)
        mine, other = pick(part[:, :HD], part[:, HD:])
        drecv[0, r, :] = mine
        dsend[r, :] = other
        return carry

    lax.fori_loop(0, 3, grad_rows, 0)
    send(dsend, drecv.at[1], s_core.at[3], r_core.at[3], sibling)
    total = attend(total, key_tiles[0])
    arrived(drecv.at[1], r_core.at[3])
    doa[y] = (drecv[0] + drecv[1]).astype(BF16)
    q_round(1)
    o_round(1)
    k_round(5)
    v_round(5)
    total = attend(total, key_tiles[1])
    q_round(2)
    o_round(2)
    total = attend(total, key_tiles[2])
    out_t = (ot[...] / total).astype(BF16).astype(F32)
    attb[c] = out_t.T.astype(BF16)
    send(attb.at[c], attb.at[c], s_core.at[4], r_core.at[4], sibling)
    lse = jnp.log2(total)
    delta = jnp.sum(out_t * own_o[...].astype(F32).T, axis=0, keepdims=True)
    for i in range(6):
        sta[slot, i:i + 1, :] = lse[:, i * HD:(i + 1) * HD]
        sta[slot, 8 + i:9 + i, :] = delta[:, i * HD:(i + 1) * HD]
    s_round(1)

    base = {4: 0, 3: SUB, 2: SUB + CH, 1: SUB + 2 * CH}

    def rs_step(n, partial, j):
        if j == 4:
            pbuf[:CH, :] = partial([rows_of(lax.rem(z + 4, 8), 0, CH)])
        else:
            pbuf[...] = partial([rows_of(lax.rem(z + sign * j + 8, 8), 0, CH) for sign in (1, -1)])
        for h in range(2):
            for i, sign in enumerate((1, -1)):
                if j == 4 and h != i:
                    continue
                first = h * SUB + (0 if j == 4 else i * CH)
                value = pbuf[first:first + SUB, :]
                r = pl.ds(0 if j == 4 else base[j] + h * SUB, SUB)
                k = (j - 1) * 4 + i * 2 + h
                if j < 3 or (j == 3 and h == i):
                    prev = pl.ds(0 if j == 3 else base[j + 1] + h * SUB, SUB)
                    arrived(rrcv.at[n, i, prev], r_rs.at[n, k + 4])
                    value = value + rrcv[n, i, prev, :].astype(F32)
                rsnd[n, i, r, :] = value.astype(BF16)
                send(rsnd.at[n, i, r], rrcv.at[n, i, r], s_rs.at[n, k], r_rs.at[n, k], at_z(z + sign))

    def rs_finish(n, partial):
        pbuf[:CH, :] = partial([rows_of(z, 0, CH)])
        cols = pl.ds(pl.multiple_of(c * HALF, 128), HALF)
        for sub in range(2):
            value = pbuf[sub * SUB:(sub + 1) * SUB, :]
            r = pl.ds(base[1] + sub * SUB, SUB)
            for i in range(2):
                arrived(rrcv.at[n, i, r], r_rs.at[n, i * 2 + sub])
                value = value + rrcv[n, i, r, :].astype(F32)
            rfin[n, sub * SUB:(sub + 1) * SUB, :] = value.astype(BF16)
            src = rfin.at[n, pl.ds(sub * SUB, SUB)]
            dst = ret.at[n, :, cols]
            here = jnp.logical_and(own, yh == sub)

            @pl.when(here)
            def _():
                pltpu.make_async_copy(src, dst, r_ret.at[n, c]).start()

            copy = remote(src, dst, s_ret.at[n, sub], r_ret.at[n, c], dev(yh=sub, c=yh))

            @pl.when(jnp.logical_not(here))
            def _():
                copy.start()

            def done(here=here, copy=copy):
                @pl.when(jnp.logical_not(here))
                def _():
                    copy.wait_send()
            pending.append(done)

    def ret_wait(n):
        for h in range(2):
            dst = ret.at[n, :, h * HALF:(h + 1) * HALF]
            pltpu.make_async_copy(dst, dst, r_ret.at[n, h]).wait()

    def stack(ref, spans):
        return jnp.concatenate(
            [jnp.concatenate([ref[0, r, :], ref[1, r, :]], axis=1) for r in spans], axis=0
        )

    def proj_part(spans):
        return dot(stack(attb, spans), wo[...])

    def dmod_part(spans):
        return dot(stack(dqb, spans), wq[...], NT)

    def backward(kref, vref, qref, oref, valid, lse, delta, to_query, to_key, first=False):
        def block(t, carry):
            r = pl.ds(pl.multiple_of(t * 256, 256), 256)
            keys_ = kref[r, :]
            query_ = qref[...]
            grad_ = oref[...]
            p = jnp.exp2(scores(keys_, query_) - lse) * valid
            d_prob = dot(vref[r, :], grad_, NT)
            ds = (p * (d_prob - delta)).astype(BF16)
            if to_query:
                dqt[...] += dot(keys_, ds, TN)
            if to_key:
                new_v = dot(p.astype(BF16), grad_)
                new_k = dot(ds, query_)
                if first:
                    dv[r, :] = new_v
                    dk[r, :] = new_k
                else:
                    dv[r, :] += new_v
                    dk[r, :] += new_k
            return carry
        lax.fori_loop(0, 3, block, 0)

    dqt[...] = jnp.zeros_like(dqt)
    arrived(attb.at[1 - c], r_core.at[4])
    rs_step(0, proj_part, 4)
    q_round(3)
    o_round(3)
    s_round(2)
    backward(own_k, own_v, own_q, own_o, one, lse, delta, True, True, True)
    rs_step(0, proj_part, 3)
    q_round(4)
    o_round(4)
    s_round(3)
    backward(nk.at[0], nv.at[0], own_q, own_o, key_tiles[1][2], lse, delta, True, False)
    rs_step(0, proj_part, 2)
    s_round(4)
    backward(nk.at[1], nv.at[1], own_q, own_o, key_tiles[2][2], lse, delta, True, False)
    rs_step(0, proj_part, 1)
    q_round(5)
    o_round(5)
    s_round(5)

    def from_stats(s, first):
        return jnp.concatenate([sta[s, first + i:first + i + 1, :] for i in range(6)], axis=1)

    q_, o_, s, valid = query_tiles[0]
    backward(own_k, own_v, q_, o_, valid, from_stats(s, 0), from_stats(s, 8), False, True)
    q_, o_, s, valid = query_tiles[1]
    backward(own_k, own_v, q_, o_, valid, from_stats(s, 0), from_stats(s, 8), False, True)
    rs_finish(0, proj_part)

    def through_norm(source, grad, row):
        r = lax.rsqrt(jnp.mean(source * source, axis=-1, keepdims=True) + EPS)
        g = grad * gains[row:row + 1, :]
        return r * g - source * (r * r * r) * jnp.mean(source * g, axis=-1, keepdims=True)

    dqt_rows = drecv
    dqt_rows[0] = dqt[...].T * FACTOR

    def norm_back(t, carry):
        r = pl.ds(pl.multiple_of(t * 256, 256), 256)
        rows = raw[r, :]
        dqb[c, r, :HD] = through_norm(rows[:, :HD], dqt_rows[0, r, :], 0).astype(BF16)
        dqb[c, r, HD:2 * HD] = through_norm(rows[:, HD:2 * HD], dk[r, :] * FACTOR, 1).astype(BF16)
        dqb[c, r, 2 * HD:] = dv[r, :].astype(BF16)
        return carry

    lax.fori_loop(0, 3, norm_back, 0)
    send(dqb.at[c], dqb.at[c], s_core.at[5], r_core.at[5], sibling)
    arrived(dqb.at[1 - c], r_core.at[5])
    rs_step(1, dmod_part, 4)
    rs_step(1, dmod_part, 3)
    ret_wait(0)
    res_out[...] = (hid[...].astype(F32) + gate * ret[0].astype(F32)).astype(BF16)
    rs_step(1, dmod_part, 2)
    rs_step(1, dmod_part, 1)
    rs_finish(1, dmod_part)
    hat, r = normed()
    ret_wait(1)
    g = ret[1].astype(F32) * (1.0 + scale)
    d_in = r * (g - jnp.mean(g, axis=-1, keepdims=True) - hat * jnp.mean(g * hat, axis=-1, keepdims=True))
    gh_out[...] = (cot[...].astype(F32) + d_in).astype(BF16)

    for done in pending:
        done()
    for t in range(3):
        r = pl.ds(t * 256, 256)
        remote(psend.at[r], precv.at[r], s_core.at[t], r_core.at[t], sibling).wait_send()


def per_device(hidden, cotangent, step_index, mod_table, w_qkv, qk_gains, w_out, tile_pairs, tile_owner):
    vm = pl.BlockSpec(memory_space=pltpu.VMEM)
    sm = pl.BlockSpec(memory_space=pltpu.SMEM)
    hbm = pl.BlockSpec(memory_space=pl.ANY)
    dma = pltpu.SemaphoreType.DMA
    V = pltpu.VMEM
    return pl.pallas_call(
        kernel,
        out_shape=[jax.ShapeDtypeStruct(hidden.shape, BF16)] * 2,
        in_specs=[vm, vm, sm, vm, hbm, vm, hbm, sm, sm],
        out_specs=[vm, vm],
        scratch_shapes=[
            V((SUB, D), BF16), V((SUB, D), BF16), V((TILE, HALF), BF16), V((TILE, HALF), BF16),
            V((HALF, 768), BF16), V((256, HALF), BF16), V((TILE, 384), F32), V((TILE, 384), F32), V((TILE, 384), F32),
            V((TILE, HD), F32), V((2, TILE, HD), F32),
            *[V((4, TILE, HD), BF16)] * 4,
            V((16, 16, HD), F32), V((2, TILE, HD), BF16), V((2, TILE, 384), BF16),
            V((HD, TILE), F32), V((HD, TILE), F32), V((TILE, HD), F32), V((TILE, HD), F32),
            V((2, 2, 336, HALF), BF16), V((2, 2, 336, HALF), BF16), V((2, CH, HALF), BF16), V((2, SUB, D), BF16), V((2 * CH, HALF), F32),
            *[V((2, TILE, HD), BF16)] * 4, *[V((2, 2, TILE, HD), BF16)] * 4,
            V((4, 2, 2, TILE, HD), BF16), V((4, 2, 2, 2, HALF_T, HD), BF16), pltpu.SMEM((16,), jnp.int32),
            dma((2, 2)), dma((2, 2)), dma((2, 5)), dma((2, 5)), dma((2,)), dma((2, 16)), dma((2, 16)), dma((6,)), dma((6,)),
            dma((5, 20)), dma((5, 20)), dma((2, 16)), dma((2, 16)), dma((2, 2)), dma((2, 2)),
        ],
        compiler_params=pltpu.CompilerParams(
            collective_id=0, has_side_effects=True, vmem_limit_bytes=60 * 2 ** 20
        ),
        name="sublayer",
    )(
        hidden, cotangent, step_index, jnp.transpose(mod_table, (1, 0, 2)), w_qkv.reshape(D, 384),
        qk_gains, w_out.reshape(HD, D), tile_pairs.T, tile_owner,
    )


def solution(mesh):
    rows = P(("blk", "head"), None)
    in_specs = (
        rows, rows, P(), P(), P(None, "head", None), P(), P("head", None, None), P(), P(),
    )
    return jax.shard_map(
        per_device, mesh=mesh, in_specs=in_specs, out_specs=(rows, rows), check_vma=False
    )
```
